32 devices in a mesh: pair: 4 (over y, x), ep: 8 (over z, core).
Axes of the slice: x: 2, y: 2, z: 4, core: 2. Of those that a mesh axis runs over, the one named last changes fastest.
Arguments:
- hidden: float32 [4, 256, 2048], P('pair', 'ep'), may hold values from -6 to 6
- moe_gain: float32 [2048], replicated, may hold values from 0.25 to 1.75
- expert_ids: int32 [4, 256, 2], P('pair', 'ep'), may hold values from 0 to 3, all different within a row; in each aligned block of 32 rows (0 to 31, 32 to 63, ..., all dimensions but the last counted through in order) at most 32 rows name the same one
- gate_weights: float32 [4, 256, 2], P('pair', 'ep'), may hold values from 0.2 to 1
- w_gate: bfloat16 [8, 2048, 2048], P('ep', None, 'pair'), may hold values from -0.125 to 0.125
- w_up: bfloat16 [8, 2048, 2048], P('ep', None, 'pair'), may hold values from -0.125 to 0.125
- w_down: bfloat16 [8, 2048, 2048], P('ep', 'pair'), may hold values from -0.09375 to 0.09375
- final_gain: float32 [2048], replicated, may hold values from 0.25 to 1.75
- w_out: bfloat16 [2048, 128], replicated, may hold values from -0.125 to 0.125
- latent: float32 [4, 256, 64], P('pair', 'ep'), may hold values from -6 to 6
- w_in: bfloat16 [128, 2048], replicated, may hold values from -0.5 to 0.5
- modulation: float32 [4, 2, 2048], P('pair'), may hold values from -3 to 16, as said below
- w_qkv: bfloat16 [2048, 3072], P(None, 'pair'), may hold values from -0.125 to 0.125
Outputs:
- latent_next: float32 [4, 256, 64], P('pair', 'ep')
- attended: bfloat16 [4, 256, 1024], P('pair', 'ep')
The draws below stay inside these ranges and needn't reach their ends.
Inputs may be any that keep to these rules, and one draw needn't show every extreme that they name: `expert_ids`: within the 32 frames of each device no expert is named more than 32 times, a bound that some block reaches; the two experts of a frame differ. `modulation`: row 0 is a shift, row 1 a positive scale.
All inputs are finite; a program needn't handle non-finite values.
Results may differ from the reference program's by a relative error of at most 0.03.
Values may be sent and summed in bfloat16 or wider, within the bound.
A program may use at most 64 MiB of HBM per device.

```python
import math
import jax
import jax.numpy as jnp
import numpy as np
from jax import lax

D = 2048
HID = 4096
HEADS = 8
HDIM = 128
CH = 64
TOK_DEV = 32
EXPERTS = 4
CAP = 32
GROUPS = 4
FRAMES = 256
C = 128
HD = 1024
N_PAIR = 4
N_EP = 8


def draw_modulation(key, part):
    shift_key, scale_key = jax.random.split(jax.random.fold_in(key, 17))
    shift_row = jnp.clip(0.5 * jax.random.normal(shift_key, (GROUPS, 1, D), jnp.float32), -3.0, 3.0)
    scale_row = jnp.exp(jax.random.uniform(scale_key, (GROUPS, 1, D), jnp.float32, math.log(0.5), math.log(2.0)))
    return jnp.concatenate([shift_row, scale_row], 1)


def level_of(rng, extent, shards, least, top_value):
    def one(position, shards_of):
        steps = jax.random.uniform(jax.random.fold_in(jax.random.fold_in(rng, 6), position), (shards_of,), jnp.float32, least / len(shards), top_value / len(shards))
        return jnp.repeat(jnp.exp(steps), extent[position] // shards_of).reshape((-1,) + (1,) * (len(extent) - position - 1))

    loudness = one(*shards[0])
    for cut in shards[1:]:
        loudness = loudness * one(*cut)
    return loudness


def assign_block(rng, own, number, rows, number_of, top, most, lean):
    ranking = jax.random.permutation(rng, number_of)
    heavy_load, usual = load_shares(number_of, rows * top, most, lean, True), load_shares(number_of, rows * top, most, lean, False)
    places = jnp.arange(number_of)

    def named(tallies, rotation):
        used = int((tallies > 0).sum())
        fixed = max(1, used // 4)
        shifted = fixed + (places - fixed + rotation * (used - fixed)) % max(1, number_of - fixed)
        return jnp.zeros((number_of,), jnp.int32).at[ranking[jnp.where(places < fixed, places, shifted)]].set(jnp.asarray(tallies, jnp.int32))

    tallies = jnp.where(number % 4 == 0, named(heavy_load, number // 4), named(usual, number - number // 4 - 1))
    mixed = jax.random.permutation(jax.random.fold_in(own, 3), number_of)
    giver, receiver = mixed[0:number_of // 2 * 2:2], mixed[1:number_of // 2 * 2:2]
    room = jnp.minimum(tallies[giver] - 1, most - tallies[receiver]) // 2
    room = jnp.where((giver == ranking[0]) | (receiver == ranking[0]) | (tallies[receiver] == 0), 0, jnp.maximum(room, 0))
    shifted = jax.random.randint(jax.random.fold_in(own, 4), (number_of // 2,), 0, 1 << 20) % (room + 1)
    tallies = tallies.at[giver].add(-shifted).at[receiver].add(shifted)
    labels = jnp.searchsorted(jnp.cumsum(tallies), jnp.arange(rows * top), side="right").astype(jnp.int32)
    table = labels.reshape(top, rows).T
    table = table[jax.random.permutation(jax.random.fold_in(own, 1), rows)]
    rotation = jax.random.randint(jax.random.fold_in(own, 2), (rows, 1), 0, top)
    return jnp.take_along_axis(table, (jnp.arange(top)[None, :] + rotation) % top, axis=1)


def load_shares(number_of, total, reach, skew, full):
    weights = [(1 << 20) // math.isqrt(rank ** skew) + 1 for rank in range(1, number_of + 1)]
    largest = reach if full else min(reach, max(-(-total // number_of), total * weights[0] // sum(weights)))
    least = 1 if total - largest >= number_of - 1 else 0
    holding, spare = [largest] + [least] * (number_of - 1), total - largest - least * (number_of - 1)
    while spare > 0:
        movable = [i for i in range(1, number_of) if holding[i] < largest] or [i for i in range(1, number_of) if holding[i] < reach]
        mass, left = sum([weights[i] for i in movable]), spare
        for i in movable:
            extra = min(reach - holding[i], max(1, left * weights[i] // mass), spare)
            holding[i] = holding[i] + extra
            spare = spare - extra
    return np.array(holding)


def scatter_about(own_key, extent, width, bound, shards=(), held_as=jnp.bfloat16):
    entries = width * jax.random.normal(own_key, extent, jnp.float32)
    if shards:
        entries = entries * level_of(own_key, extent, shards, -0.22, 0.18)
    return jnp.clip(entries, -bound, bound).astype(held_as)


def setup_inputs(seed: int = 0) -> dict:
    arg_keys = jax.random.split(jax.random.key(seed), 14)
    hidden = scatter_about(arg_keys[0], (GROUPS, FRAMES, D), 1.0, 6.0, ((0, 4), (1, 8)), jnp.float32)
    moe_gain = jnp.clip(1.0 + 0.15 * jax.random.normal(arg_keys[1], (D,), jnp.float32), 0.25, 1.75)
    expert_ids_keys = jax.random.split(jax.random.fold_in(arg_keys[2], 1), GROUPS * FRAMES // TOK_DEV)
    expert_ids_turns = jax.random.permutation(jax.random.fold_in(arg_keys[2], 3), GROUPS * FRAMES // TOK_DEV)
    expert_ids = jax.vmap(lambda own, number: assign_block(jax.random.fold_in(arg_keys[2], 2), own, number, TOK_DEV, EXPERTS, 2, CAP, 2))(expert_ids_keys, expert_ids_turns).reshape((GROUPS, FRAMES, 2))
    gate_weights = jnp.clip(0.2 + 0.8 * jax.random.uniform(arg_keys[3], (GROUPS, FRAMES, 2), jnp.float32) ** level_of(arg_keys[3], (GROUPS, FRAMES, 2), ((0, 4), (1, 8)), -0.2, 0.2), 0.2, 1.0)
    w_gate = scatter_about(arg_keys[4], (2 * EXPERTS, D, HID // 2), D ** -0.5, 0.125, ((0, 8), (2, 4)))
    w_up = scatter_about(arg_keys[5], (2 * EXPERTS, D, HID // 2), D ** -0.5, 0.125, ((0, 8), (2, 4)))
    w_down = scatter_about(arg_keys[6], (2 * EXPERTS, HID // 2, D), HID ** -0.5, 0.09375, ((0, 8), (1, 4)))
    final_gain = jnp.clip(1.0 + 0.15 * jax.random.normal(arg_keys[7], (D,), jnp.float32), 0.25, 1.75)
    w_out = scatter_about(arg_keys[8], (D, C), D ** -0.5, 0.125)
    latent = scatter_about(arg_keys[9], (GROUPS, FRAMES, CH), 1.0, 6.0, ((0, 4), (1, 8)), jnp.float32)
    w_in = scatter_about(arg_keys[10], (C, D), C ** -0.5, 0.5)
    modulation = draw_modulation(jax.random.fold_in(arg_keys[13], 71), 0)
    w_qkv = scatter_about(arg_keys[12], (D, 3 * HD), D ** -0.5, 0.125, ((1, 4),))
    return dict(hidden=hidden, moe_gain=moe_gain, expert_ids=expert_ids, gate_weights=gate_weights, w_gate=w_gate, w_up=w_up, w_down=w_down, final_gain=final_gain, w_out=w_out, latent=latent, w_in=w_in, modulation=modulation, w_qkv=w_qkv)


EPSILON = 1e-06
GUIDANCE = 3.0
STEP_SIZE = 0.25

def rms_scale(values):
    return values * lax.rsqrt(lax.optimization_barrier(jnp.mean(values * values, -1, keepdims=True)) + EPSILON)

def expert_half(block_rows, gate_mat, up_mat, down_mat):
    quarter = gate_mat.shape[1] // N_PAIR
    gated = jnp.dot(block_rows, gate_mat, preferred_element_type=jnp.float32)
    upward = jnp.dot(block_rows, up_mat, preferred_element_type=jnp.float32)
    active = (jax.nn.silu(gated) * upward).astype(jnp.bfloat16)
    partial_sums = jnp.einsum('rqs,qsd->qrd', active.reshape(block_rows.shape[0], N_PAIR, quarter).astype(jnp.float32), down_mat.reshape(N_PAIR, quarter, D).astype(jnp.float32), precision=lax.Precision.HIGHEST)
    rounded = lax.optimization_barrier(partial_sums.astype(jnp.bfloat16))
    return lax.optimization_barrier(jnp.sum(rounded.astype(jnp.float32), 0)).astype(jnp.bfloat16)

def group_velocity(hidden_row, ids_row, gates_row, moe_gain, w_gate, w_up, w_down, final_gain, w_out):
    experts = N_EP // 2
    capacity = 4 * TOK_DEV // experts
    slot_total = N_EP * capacity
    normed = (rms_scale(hidden_row) * moe_gain).astype(jnp.bfloat16)
    flat_ids = ids_row.reshape(N_EP, TOK_DEV * 2).astype(jnp.int32)
    onehot = (flat_ids[:, :, None] == jnp.arange(experts, dtype=jnp.int32)[None, None, :]).astype(jnp.int32)
    slot_rank = lax.optimization_barrier(jnp.sum((jnp.cumsum(onehot, 1) - onehot) * onehot, -1)).astype(jnp.int32)
    sources = jnp.arange(N_EP, dtype=jnp.int32)[:, None]
    places = (flat_ids * slot_total + sources * capacity + slot_rank).reshape(-1).astype(jnp.int32)
    frame_ids = jnp.repeat(jnp.arange(FRAMES, dtype=jnp.int32), 2)
    table = jnp.full((experts * slot_total,), FRAMES, jnp.int32).at[places].set(frame_ids)
    padded = jnp.concatenate([normed, jnp.zeros((1, D), jnp.bfloat16)], 0)

    def run_expert(expert):
        picks = lax.dynamic_slice_in_dim(table, expert * slot_total, slot_total)
        block_rows = padded[picks]
        first_half = expert_half(block_rows, w_gate[2 * expert], w_up[2 * expert], w_down[2 * expert])
        second_half = expert_half(block_rows, w_gate[2 * expert + 1], w_up[2 * expert + 1], w_down[2 * expert + 1])
        return first_half.astype(jnp.float32) + second_half.astype(jnp.float32)
    summed = lax.map(run_expert, jnp.arange(experts, dtype=jnp.int32)).reshape(experts * slot_total, D)
    mixed_out = (gates_row.reshape(-1)[:, None] * summed[places]).reshape(FRAMES, 2, D).sum(1)
    resid = hidden_row + mixed_out
    return jnp.dot((rms_scale(resid) * final_gain).astype(jnp.bfloat16), w_out, preferred_element_type=jnp.float32)

def attend(advanced, modulation_row, w_in, w_qkv):
    embedded = jnp.dot(advanced.astype(jnp.bfloat16), w_in, preferred_element_type=jnp.float32)
    modulated = (rms_scale(embedded) * modulation_row[1] + modulation_row[0]).astype(jnp.bfloat16)
    projected = jnp.dot(modulated, w_qkv, preferred_element_type=jnp.float32).astype(jnp.bfloat16)
    head_width = HEADS * HDIM
    queries = projected[:, :head_width].reshape(FRAMES, HEADS, HDIM).astype(jnp.float32)
    key_cols = projected[:, head_width:2 * head_width].reshape(FRAMES, HEADS, HDIM).astype(jnp.float32)
    value_cols = projected[:, 2 * head_width:].reshape(FRAMES, HEADS, HDIM).astype(jnp.float32)
    score_scale = 1.0 / math.sqrt(HDIM)
    scores = jnp.einsum('thd,nhd->htn', queries, key_cols, precision=lax.Precision.HIGHEST) * score_scale
    weights = jax.nn.softmax(scores, -1)
    output = jnp.einsum('htn,nhd->thd', weights, value_cols, precision=lax.Precision.HIGHEST)
    return output.reshape(FRAMES, head_width).astype(jnp.bfloat16)

def reference(hidden, moe_gain, expert_ids, gate_weights, w_gate, w_up, w_down, final_gain, w_out, latent, w_in, modulation, w_qkv):
    velocities = [group_velocity(hidden[member], expert_ids[member], gate_weights[member], moe_gain, w_gate, w_up, w_down, final_gain, w_out) for member in range(N_PAIR)]
    next_rows = []
    attended_rows = []
    for member in range(N_PAIR):
        leader = member - member % 2
        cond_vel = velocities[leader]
        uncond_vel = velocities[leader + 1]
        guided = uncond_vel + GUIDANCE * (cond_vel - uncond_vel)
        advanced = jnp.concatenate([latent[leader], latent[leader + 1]], -1) + STEP_SIZE * guided
        half_index = member % 2
        next_rows.append(advanced[:, half_index * CH:(half_index + 1) * CH])
        attended_rows.append(attend(advanced, modulation[member], w_in, w_qkv))
    return (jnp.stack(next_rows), jnp.stack(attended_rows))
```

```python
import math

import jax
import jax.numpy as jnp
from jax import lax
from jax.experimental import pallas as pl
from jax.experimental.pallas import tpu as pltpu
from jax.sharding import PartitionSpec as P

HDIM = 128


EPSILON = 1e-06
GUIDANCE = 3.0
STEP_SIZE = 0.25


def from_partner(value, axis, bit):
    mask = 2**bit
    pairs = [(source, source ^ mask) for source in range(lax.axis_size(axis))]
    return lax.ppermute(value, axis, pairs)


def rms_scale(values):
    return values * lax.rsqrt(jnp.mean(values * values, -1, keepdims=True) + EPSILON)


def per_device(
    hidden,
    moe_gain,
    expert_ids,
    gate_weights,
    w_gate,
    w_up,
    w_down,
    final_gain,
    w_out,
    latent,
    w_in,
    modulation,
    w_qkv,
):
    tok_rows = hidden.shape[1]
    model_width = hidden.shape[2]
    experts = lax.axis_size("ep") // 2
    capacity = 4 * tok_rows // experts
    slot_count = experts * capacity
    own_hidden = hidden[0]
    normed = (rms_scale(own_hidden) * moe_gain).astype(jnp.bfloat16)
    flat_ids = expert_ids[0].reshape(-1)
    onehot = (flat_ids[:, None] == jnp.arange(experts, dtype=jnp.int32)[None, :]).astype(jnp.int32)
    slot_rank = jnp.sum((jnp.cumsum(onehot, 0) - onehot) * onehot, 1)
    places = flat_ids * capacity + slot_rank
    matches = places[None, :] == jnp.arange(slot_count, dtype=jnp.int32)[:, None]
    dispatch_mat = jnp.sum(matches.reshape(slot_count, tok_rows, 2).astype(jnp.float32), 2).astype(
        jnp.bfloat16
    )
    buffers = jnp.dot(dispatch_mat, normed, preferred_element_type=jnp.float32).astype(jnp.bfloat16)
    doubled = jnp.broadcast_to(
        buffers.reshape(experts, 1, capacity, model_width), (experts, 2, capacity, model_width)
    ).reshape(2 * experts, capacity, model_width)
    arrived = lax.all_to_all(doubled, "ep", split_axis=0, concat_axis=0, tiled=True)
    all_rows = lax.all_gather(arrived.reshape(-1, model_width), "pair", axis=0, tiled=True)
    gate_mat = w_gate[0]
    up_mat = w_up[0]
    down_mat = w_down[0]
    gated = jnp.dot(all_rows, gate_mat, preferred_element_type=jnp.float32)
    upward = jnp.dot(all_rows, up_mat, preferred_element_type=jnp.float32)
    active = (jax.nn.silu(gated) * upward).astype(jnp.bfloat16)
    halves = lax.psum_scatter(
        jnp.dot(active, down_mat, preferred_element_type=jnp.float32).astype(jnp.bfloat16),
        "pair",
        scatter_dimension=0,
        tiled=True,
    )
    returned = lax.all_to_all(
        halves.reshape(2 * experts, capacity, model_width),
        "ep",
        split_axis=0,
        concat_axis=0,
        tiled=True,
    )
    paired = returned.reshape(experts, 2, capacity, model_width)
    summed = (paired[:, 0].astype(jnp.float32) + paired[:, 1].astype(jnp.float32)).reshape(
        slot_count, model_width
    )
    combine_mat = jnp.sum(
        jnp.where(matches, gate_weights[0].reshape(-1)[None, :], 0.0).reshape(
            slot_count, tok_rows, 2
        ),
        2,
    )
    mixed_out = jnp.einsum("st,sd->td", combine_mat, summed, precision=lax.Precision.HIGHEST)
    resid = own_hidden + mixed_out
    velocity = jnp.dot(
        (rms_scale(resid) * final_gain).astype(jnp.bfloat16),
        w_out,
        preferred_element_type=jnp.float32,
    )
    own_latent = latent[0]
    outgoing = jnp.concatenate([velocity, own_latent], 1)
    incoming = from_partner(outgoing, "pair", 0)
    channels = velocity.shape[1]
    partner_vel = incoming[:, :channels]
    partner_latent = incoming[:, channels:]
    is_cond = lax.axis_index("pair") % 2 == 0
    cond_vel = jnp.where(is_cond, velocity, partner_vel)
    uncond_vel = jnp.where(is_cond, partner_vel, velocity)
    guided = uncond_vel + GUIDANCE * (cond_vel - uncond_vel)
    whole_latent = jnp.where(
        is_cond,
        jnp.concatenate([own_latent, partner_latent], 1),
        jnp.concatenate([partner_latent, own_latent], 1),
    )
    advanced = whole_latent + STEP_SIZE * guided
    half_width = own_latent.shape[1]
    own_next = jnp.where(is_cond, advanced[:, :half_width], advanced[:, half_width:])
    embedded = jnp.dot(advanced.astype(jnp.bfloat16), w_in, preferred_element_type=jnp.float32)
    modulated = (rms_scale(embedded) * modulation[0, 1] + modulation[0, 0]).astype(jnp.bfloat16)
    all_modulated = lax.all_gather(modulated, "pair", axis=0, tiled=True)
    local_cols = jnp.dot(all_modulated, w_qkv, preferred_element_type=jnp.float32).astype(
        jnp.bfloat16
    )
    projected = lax.all_to_all(local_cols, "pair", split_axis=0, concat_axis=1, tiled=True)
    head_width = projected.shape[1] // 3
    head_count = head_width // HDIM
    queries = projected[:, :head_width].reshape(tok_rows, head_count, HDIM)
    key_cols = projected[:, head_width : 2 * head_width]
    value_cols = projected[:, 2 * head_width :]
    score_scale = 1.0 / math.sqrt(HDIM)
    running_max = jnp.full((head_count, tok_rows), -1e30, jnp.float32)
    key_piece = lax.all_gather(key_cols, "ep", axis=0, tiled=True).reshape(-1, head_count, HDIM)
    value_piece = lax.all_gather(value_cols, "ep", axis=0, tiled=True).reshape(-1, head_count, HDIM)
    scores = (
        jnp.einsum("thd,nhd->htn", queries, key_piece, preferred_element_type=jnp.float32)
        * score_scale
    )
    new_max = jnp.maximum(running_max, jnp.max(scores, 2))
    weights = jnp.exp(scores - new_max[:, :, None])
    new_sum = jnp.sum(weights, 2)
    new_accum = jnp.einsum(
        "htn,nhd->htd", weights, value_piece.astype(jnp.float32), precision=lax.Precision.HIGHEST
    )
    attended = (
        (new_accum / new_sum[:, :, None])
        .transpose(1, 0, 2)
        .reshape(tok_rows, head_width)
        .astype(jnp.bfloat16)
    )
    return (own_next[None], attended[None])


Z_IN, X_IN, Y_IN, XY_IN, YX_IN, CORE_IN = 0, 1, 2, 3, 4, 5
CORE_OUT, XD_OUT, YD_OUT, X_OUT, Y_OUT, Z_OUT = 9, 10, 11, 12, 13, 14
KINDS = 15


def fused_kernel(
    hid,
    moe_gain,
    ids,
    gates,
    gate_hbm,
    up_hbm,
    down_hbm,
    final_gain,
    out_hbm,
    lat,
    in_hbm,
    mod,
    qkv_hbm,
    next_ref,
    att_ref,
    rows,
    wg,
    wu,
    wd,
    wout,
    win,
    wqkv,
    act,
    sums,
    core_send,
    core_recv,
    diag_send,
    diag_recv,
    side_send,
    side_recv,
    z_send,
    z_recv,
    lats,
    mods,
    vels,
    cols,
    qkv,
    heads,
    whole,
    load_sem,
    send_sem,
    recv_sem,
    small_send,
    small_recv,
    col_send,
    col_recv,
    head_send,
    head_recv,
):
    p, ep = lax.axis_index("pair"), lax.axis_index("ep")
    x, y = lax.rem(p, 2), lax.div(p, 2)
    core, z = lax.rem(ep, 2), lax.div(ep, 2)
    px, py = y * 2 + (1 - x), (1 - y) * 2 + x
    pd = (1 - y) * 2 + (1 - x)
    pairs = (p, px, py, pd)
    core_ep = z * 2 + (1 - core)
    tok = hid.shape[1]
    half = tok // 2
    hidden_units = wg.shape[1]
    width = wd.shape[1]

    def place(k):
        low = lax.rem(lax.rem(z, 2) + lax.rem(k, 2), 2)
        high = lax.rem(lax.div(z, 2) + lax.div(k, 2), 2)
        return high * 2 + low

    def copy(src, dst, sent, received, device):
        return pltpu.make_async_remote_copy(
            src_ref=src,
            dst_ref=dst,
            send_sem=sent,
            recv_sem=received,
            device_id=device,
            device_id_type=pl.DeviceIdType.MESH,
        )

    top, low = pl.ds(0, half), pl.ds(half, half)

    def group(kind, k):
        if kind == Z_IN:
            src, dst, dev = rows.at[0, 0, 0], rows.at[k, 0, 0], (p, place(k) * 2 + core)
        elif kind == X_IN:
            src, dst, dev = rows.at[k, 0, 0], rows.at[k, 0, 1], (px, ep)
        elif kind == Y_IN:
            src, dst, dev = rows.at[k, 0, 0], rows.at[k, 0, 2], (py, ep)
        elif kind == XY_IN:
            src, dst, dev = rows.at[k, 0, 1, top], rows.at[k, 0, 3, top], (py, ep)
        elif kind == YX_IN:
            src, dst, dev = rows.at[k, 0, 2, low], rows.at[k, 0, 3, low], (px, ep)
        elif kind < CORE_OUT:
            r = kind - CORE_IN
            src, dst, dev = rows.at[k, 0, r], rows.at[k, 1, r], (p, core_ep)
        elif kind == CORE_OUT:
            src, dst, dev = core_send.at[k], core_recv.at[k], (p, core_ep)
        elif kind == XD_OUT:
            src, dst, dev = diag_send.at[k, 0], diag_recv.at[k, 0], (px, ep)
        elif kind == YD_OUT:
            src, dst, dev = diag_send.at[k, 1], diag_recv.at[k, 1], (py, ep)
        elif kind == X_OUT:
            src, dst, dev = side_send.at[k, 0], side_recv.at[k, 0], (px, ep)
        elif kind == Y_OUT:
            src, dst, dev = side_send.at[k, 1], side_recv.at[k, 1], (py, ep)
        else:
            src, dst, dev = z_send.at[k], z_recv.at[k], (p, place(k) * 2 + core)
        return copy(src, dst, send_sem.at[kind, k], recv_sem.at[kind, k], dev)

    loads = [
        pltpu.make_async_copy(src, dst, load_sem.at[i])
        for i, (src, dst) in enumerate(
            (
                (gate_hbm.at[0], wg),
                (up_hbm.at[0], wu),
                (down_hbm.at[0], wd),
                (out_hbm, wout),
                (in_hbm, win),
                (qkv_hbm, wqkv),
            )
        )
    ]

    rows[0, 0, 0] = (rms_scale(hid[0]) * moe_gain[...]).astype(jnp.bfloat16)
    for k in range(1, 4):
        group(Z_IN, k).start()
    for load in loads:
        load.start()
    lats[0] = jnp.zeros_like(lats[0])
    lats[0, :, : lat.shape[2]] = lat[0]
    mods[0] = mod[0]

    def small(kind, r):
        buffer = (lats, mods, vels)[kind]
        return copy(
            buffer.at[0],
            buffer.at[r],
            small_send.at[kind, r],
            small_recv.at[kind, r],
            (pairs[r], ep),
        )

    def spread(k):
        @pl.when(k > 0)
        def _():
            group(Z_IN, k).wait_recv()

        group(X_IN, k).start()
        group(Y_IN, k).start()
        group(CORE_IN, k).start()
        group(X_IN, k).wait_recv()
        group(XY_IN, k).start()
        group(CORE_IN + 1, k).start()
        group(Y_IN, k).wait_recv()
        group(YX_IN, k).start()
        group(CORE_IN + 2, k).start()

    def experts(k):
        group(XY_IN, k).wait_recv()
        group(YX_IN, k).wait_recv()
        group(CORE_IN + 3, k).start()
        for r in range(4):
            group(CORE_IN + r, k).wait_recv()

        @pl.when(k == 0)
        def _():
            for load in loads[:3]:
                load.wait()

        own = rows[k].reshape(8 * tok, width)
        step = min(256, hidden_units)
        for at in range(0, hidden_units, step):
            gated = jnp.dot(own, wg[:, at : at + step], preferred_element_type=jnp.float32)
            upward = jnp.dot(own, wu[:, at : at + step], preferred_element_type=jnp.float32)
            act[:, at : at + step] = (jax.nn.silu(gated) * upward).astype(jnp.bfloat16)
        step = min(512, width)
        for at in range(0, width, step):
            part = jnp.dot(act[...], wd[:, at : at + step], preferred_element_type=jnp.float32)
            part = part.reshape(2, 4, tok, step)
            sums[k, :, :, at : at + step] = part[0]
            core_send[k, :, :, at : at + step] = part[1].astype(jnp.bfloat16)
        group(CORE_OUT, k).start()

    def join_cores(k):
        group(CORE_OUT, k).wait_recv()
        diag = sums[k, 3] + core_recv[k, 3].astype(jnp.float32)
        diag_send[k] = diag.astype(jnp.bfloat16).reshape(2, half, width)
        group(XD_OUT, k).start()
        group(YD_OUT, k).start()
        for r in range(3):
            sums[k, r] = sums[k, r] + core_recv[k, r].astype(jnp.float32)

    def join_diagonal(k):
        group(XD_OUT, k).wait_recv()
        group(YD_OUT, k).wait_recv()
        side_send[k, 0, :half] = sums[k, 1, :half].astype(jnp.bfloat16)
        side_send[k, 0, half:] = (
            sums[k, 1, half:] + diag_recv[k, 1].astype(jnp.float32)
        ).astype(jnp.bfloat16)
        group(X_OUT, k).start()
        side_send[k, 1, :half] = (
            sums[k, 2, :half] + diag_recv[k, 0].astype(jnp.float32)
        ).astype(jnp.bfloat16)
        side_send[k, 1, half:] = sums[k, 2, half:].astype(jnp.bfloat16)
        group(Y_OUT, k).start()

    def join_sides(k):
        group(X_OUT, k).wait_recv()
        group(Y_OUT, k).wait_recv()
        total = (
            sums[k, 0]
            + side_recv[k, 0].astype(jnp.float32)
            + side_recv[k, 1].astype(jnp.float32)
        ).astype(jnp.bfloat16)

        @pl.when(k == 0)
        def _():
            z_recv[0] = total

        @pl.when(k > 0)
        def _():
            z_send[k] = total
            group(Z_OUT, k).start()

    stages = ((spread, 0), (experts, 1), (join_cores, 2), (join_diagonal, 3), (join_sides, 4))

    def turn(it, carry):
        for stage, lag in stages:

            @pl.when((it >= lag) & (it < lag + 4))
            def _(stage=stage, lag=lag):
                stage(it - lag)

        @pl.when(it == 0)
        def _():
            for r in range(1, 4):
                small(0, r).start()
                small(1, r).start()

        return carry

    lax.fori_loop(0, 8, turn, 0)

    mixed = jnp.zeros((tok, width), jnp.float32)
    for k in range(4):
        if k > 0:
            group(Z_OUT, k).wait_recv()
        weight = jnp.sum(jnp.where(ids[0] == place(k), gates[0], 0.0), 1, keepdims=True)
        mixed = mixed + weight * z_recv[k].astype(jnp.float32)
    resid = hid[0] + mixed
    loads[3].wait()
    vels[0] = jnp.dot(
        (rms_scale(resid) * final_gain[...]).astype(jnp.bfloat16),
        wout[...],
        preferred_element_type=jnp.float32,
    )
    for r in range(1, 4):
        small(2, r).start()
    for kind in range(3):
        for r in range(1, 4):
            small(kind, r).wait_recv()

    is_cond = x == 0
    half_channels = lat.shape[2]

    def advance(first, second):
        cond_vel = jnp.where(is_cond, vels[first], vels[second])
        uncond_vel = jnp.where(is_cond, vels[second], vels[first])
        cond_lat = jnp.where(is_cond, lats[first], lats[second])[:, :half_channels]
        uncond_lat = jnp.where(is_cond, lats[second], lats[first])[:, :half_channels]
        guided = uncond_vel + GUIDANCE * (cond_vel - uncond_vel)
        return jnp.concatenate([cond_lat, uncond_lat], 1) + STEP_SIZE * guided

    advanced = advance(0, 1)
    next_ref[0] = jnp.where(is_cond, advanced[:, :half_channels], advanced[:, half_channels:])
    both = jnp.concatenate([advanced, advance(2, 3)], 0).astype(jnp.bfloat16)
    loads[4].wait()
    scaled = rms_scale(jnp.dot(both, win[...], preferred_element_type=jnp.float32))
    modulated = jnp.concatenate(
        [
            (scaled[(r // 2) * tok : (r // 2 + 1) * tok] * mods[r, 1:2] + mods[r, 0:1]).astype(
                jnp.bfloat16
            )
            for r in range(4)
        ],
        0,
    )
    loads[5].wait()
    local = jnp.dot(modulated, wqkv[...], preferred_element_type=jnp.float32).astype(jnp.bfloat16)
    blocks = local.shape[1] // HDIM
    for r in range(4):
        for b in range(blocks):
            cols[r, b] = local[r * tok : (r + 1) * tok, b * HDIM : (b + 1) * HDIM]

    def column(r, b):
        number = p * blocks + b
        sort, head = lax.div(number, 8), lax.rem(number, 8)
        return head, sort, copy(
            cols.at[r, b],
            qkv.at[sort, ep],
            col_send.at[r, b],
            col_recv.at[sort, ep],
            (pairs[r], head),
        )

    def each_column(act_on, keep):
        for r in (3, 1, 2, 0):
            for b in range(blocks):
                head, sort, moved = column(r, b)
                if r > 0:
                    act_on(moved)
                    continue

                @pl.when(head != ep)
                def _(moved=moved):
                    act_on(moved)

                if keep:

                    @pl.when(head == ep)
                    def _(sort=sort, b=b):
                        qkv[sort, ep] = cols[0, b]

    each_column(lambda moved: moved.start(), True)
    for sort in range(3):
        for j in range(8):

            @pl.when((lax.div(sort * 8 + ep, blocks) != p) | (ep != j))
            def _(sort=sort, j=j):
                copy(
                    qkv.at[sort, j],
                    qkv.at[sort, j],
                    col_send.at[0, 0],
                    col_recv.at[sort, j],
                    (px, ep),
                ).wait_recv()

    query, key, value = (qkv[sort].reshape(8 * tok, HDIM) for sort in range(3))
    scores = lax.dot_general(
        query, key, (((1,), (1,)), ((), ())), preferred_element_type=jnp.float32
    ) * (1.0 / math.sqrt(HDIM))
    weights = jnp.exp(scores - jnp.max(scores, 1, keepdims=True))
    total = jnp.sum(weights, 1, keepdims=True)
    mixed_values = jnp.dot(
        weights.astype(jnp.bfloat16), value, preferred_element_type=jnp.float32
    )
    heads[...] = (mixed_values / total).astype(jnp.bfloat16).reshape(8, tok, HDIM)

    def result(d):
        j = lax.rem(ep + d, 8)
        return copy(heads.at[j], whole.at[ep], head_send.at[d], head_recv.at[d], (p, j))

    for d in range(1, 8):
        result(d).start()
    whole[ep] = heads[ep]
    for d in range(1, 8):
        j = lax.rem(ep + 8 - d, 8)
        copy(whole.at[j], whole.at[j], head_send.at[d], head_recv.at[d], (px, ep)).wait_recv()
    for h in range(8):
        att_ref[0, :, h * HDIM : (h + 1) * HDIM] = whole[h]

    def settle(k, carry):
        for kind in range(KINDS):
            if kind in (Z_IN, Z_OUT):

                @pl.when(k > 0)
                def _(kind=kind):
                    group(kind, k).wait_send()

            else:
                group(kind, k).wait_send()
        return carry

    lax.fori_loop(0, 4, settle, 0)
    for kind in range(3):
        for r in range(1, 4):
            small(kind, r).wait_send()
    each_column(lambda moved: moved.wait_send(), False)
    for d in range(1, 8):
        result(d).wait_send()


def fused(
    hidden,
    moe_gain,
    expert_ids,
    gate_weights,
    w_gate,
    w_up,
    w_down,
    final_gain,
    w_out,
    latent,
    w_in,
    modulation,
    w_qkv,
):
    tok, width = hidden.shape[1:]
    units = w_gate.shape[2]
    channels = w_out.shape[1]
    columns = w_qkv.shape[1]
    blocks = columns // HDIM
    b16, f32 = jnp.bfloat16, jnp.float32
    vmem, hbm = pl.BlockSpec(memory_space=pltpu.VMEM), pl.BlockSpec(memory_space=pl.ANY)
    dma = pltpu.SemaphoreType.DMA
    half = tok // 2
    return pl.pallas_call(
        fused_kernel,
        out_shape=(
            jax.ShapeDtypeStruct(latent.shape, f32),
            jax.ShapeDtypeStruct((1, tok, 8 * HDIM), b16),
        ),
        in_specs=[vmem] * 4 + [hbm] * 3 + [vmem, hbm, vmem, hbm, vmem, hbm],
        out_specs=(vmem, vmem),
        scratch_shapes=[
            pltpu.VMEM((4, 2, 4, tok, width), b16),
            pltpu.VMEM((width, units), b16),
            pltpu.VMEM((width, units), b16),
            pltpu.VMEM((units, width), b16),
            pltpu.VMEM(w_out.shape, b16),
            pltpu.VMEM(w_in.shape, b16),
            pltpu.VMEM(w_qkv.shape, b16),
            pltpu.VMEM((8 * tok, units), b16),
            pltpu.VMEM((4, 4, tok, width), f32),
            pltpu.VMEM((4, 4, tok, width), b16),
            pltpu.VMEM((4, 4, tok, width), b16),
            pltpu.VMEM((4, 2, half, width), b16),
            pltpu.VMEM((4, 2, half, width), b16),
            pltpu.VMEM((4, 2, tok, width), b16),
            pltpu.VMEM((4, 2, tok, width), b16),
            pltpu.VMEM((4, tok, width), b16),
            pltpu.VMEM((4, tok, width), b16),
            pltpu.VMEM((4, tok, channels), f32),
            pltpu.VMEM((4, 2, width), f32),
            pltpu.VMEM((4, tok, channels), f32),
            pltpu.VMEM((4, blocks, tok, HDIM), b16),
            pltpu.VMEM((3, 8, tok, HDIM), b16),
            pltpu.VMEM((8, tok, HDIM), b16),
            pltpu.VMEM((8, tok, HDIM), b16),
            dma((6,)),
            dma((KINDS, 4)),
            dma((KINDS, 4)),
            dma((3, 4)),
            dma((3, 4)),
            dma((4, blocks)),
            dma((3, 8)),
            dma((8,)),
            dma((8,)),
        ],
        compiler_params=pltpu.CompilerParams(
            has_side_effects=True, vmem_limit_bytes=52 * 2**20
        ),
        name="guided_step",
    )(
        hidden,
        moe_gain[None],
        expert_ids,
        gate_weights,
        w_gate,
        w_up,
        w_down,
        final_gain[None],
        w_out,
        latent,
        w_in,
        modulation,
        w_qkv,
    )


def choose(mesh):
    if mesh.shape["pair"] == 4 and mesh.shape["ep"] == 8:
        return fused
    return per_device


def solution(mesh):
    return jax.shard_map(
        choose(mesh),
        mesh=mesh,
        in_specs=(
            P("pair", "ep", None),
            P(),
            P("pair", "ep", None),
            P("pair", "ep", None),
            P("ep", None, "pair"),
            P("ep", None, "pair"),
            P("ep", "pair", None),
            P(),
            P(),
            P("pair", "ep", None),
            P(),
            P("pair", None, None),
            P(None, "pair"),
        ),
        out_specs=(P("pair", "ep", None), P("pair", "ep", None)),
        check_vma=False,
    )
```

```python
import math

import jax
import jax.numpy as jnp
from jax import lax
from jax.experimental import pallas as pl
from jax.experimental.pallas import tpu as pltpu
from jax.sharding import PartitionSpec as P

HDIM = 128


EPSILON = 1e-06
GUIDANCE = 3.0
STEP_SIZE = 0.25


def from_partner(value, axis, bit):
    mask = 2**bit
    pairs = [(source, source ^ mask) for source in range(lax.axis_size(axis))]
    return lax.ppermute(value, axis, pairs)


def rms_scale(values):
    return values * lax.rsqrt(jnp.mean(values * values, -1, keepdims=True) + EPSILON)


def per_device(
    hidden,
    moe_gain,
    expert_ids,
    gate_weights,
    w_gate,
    w_up,
    w_down,
    final_gain,
    w_out,
    latent,
    w_in,
    modulation,
    w_qkv,
):
    tok_rows = hidden.shape[1]
    model_width = hidden.shape[2]
    experts = lax.axis_size("ep") // 2
    capacity = 4 * tok_rows // experts
    slot_count = experts * capacity
    own_hidden = hidden[0]
    normed = (rms_scale(own_hidden) * moe_gain).astype(jnp.bfloat16)
    flat_ids = expert_ids[0].reshape(-1)
    onehot = (flat_ids[:, None] == jnp.arange(experts, dtype=jnp.int32)[None, :]).astype(jnp.int32)
    slot_rank = jnp.sum((jnp.cumsum(onehot, 0) - onehot) * onehot, 1)
    places = flat_ids * capacity + slot_rank
    matches = places[None, :] == jnp.arange(slot_count, dtype=jnp.int32)[:, None]
    dispatch_mat = jnp.sum(matches.reshape(slot_count, tok_rows, 2).astype(jnp.float32), 2).astype(
        jnp.bfloat16
    )
    buffers = jnp.dot(dispatch_mat, normed, preferred_element_type=jnp.float32).astype(jnp.bfloat16)
    doubled = jnp.broadcast_to(
        buffers.reshape(experts, 1, capacity, model_width), (experts, 2, capacity, model_width)
    ).reshape(2 * experts, capacity, model_width)
    arrived = lax.all_to_all(doubled, "ep", split_axis=0, concat_axis=0, tiled=True)
    all_rows = lax.all_gather(arrived.reshape(-1, model_width), "pair", axis=0, tiled=True)
    gate_mat = w_gate[0]
    up_mat = w_up[0]
    down_mat = w_down[0]
    gated = jnp.dot(all_rows, gate_mat, preferred_element_type=jnp.float32)
    upward = jnp.dot(all_rows, up_mat, preferred_element_type=jnp.float32)
    active = (jax.nn.silu(gated) * upward).astype(jnp.bfloat16)
    halves = lax.psum_scatter(
        jnp.dot(active, down_mat, preferred_element_type=jnp.float32).astype(jnp.bfloat16),
        "pair",
        scatter_dimension=0,
        tiled=True,
    )
    returned = lax.all_to_all(
        halves.reshape(2 * experts, capacity, model_width),
        "ep",
        split_axis=0,
        concat_axis=0,
        tiled=True,
    )
    paired = returned.reshape(experts, 2, capacity, model_width)
    summed = (paired[:, 0].astype(jnp.float32) + paired[:, 1].astype(jnp.float32)).reshape(
        slot_count, model_width
    )
    combine_mat = jnp.sum(
        jnp.where(matches, gate_weights[0].reshape(-1)[None, :], 0.0).reshape(
            slot_count, tok_rows, 2
        ),
        2,
    )
    mixed_out = jnp.einsum("st,sd->td", combine_mat, summed, precision=lax.Precision.HIGHEST)
    resid = own_hidden + mixed_out
    velocity = jnp.dot(
        (rms_scale(resid) * final_gain).astype(jnp.bfloat16),
        w_out,
        preferred_element_type=jnp.float32,
    )
    own_latent = latent[0]
    outgoing = jnp.concatenate([velocity, own_latent], 1)
    incoming = from_partner(outgoing, "pair", 0)
    channels = velocity.shape[1]
    partner_vel = incoming[:, :channels]
    partner_latent = incoming[:, channels:]
    is_cond = lax.axis_index("pair") % 2 == 0
    cond_vel = jnp.where(is_cond, velocity, partner_vel)
    uncond_vel = jnp.where(is_cond, partner_vel, velocity)
    guided = uncond_vel + GUIDANCE * (cond_vel - uncond_vel)
    whole_latent = jnp.where(
        is_cond,
        jnp.concatenate([own_latent, partner_latent], 1),
        jnp.concatenate([partner_latent, own_latent], 1),
    )
    advanced = whole_latent + STEP_SIZE * guided
    half_width = own_latent.shape[1]
    own_next = jnp.where(is_cond, advanced[:, :half_width], advanced[:, half_width:])
    embedded = jnp.dot(advanced.astype(jnp.bfloat16), w_in, preferred_element_type=jnp.float32)
    modulated = (rms_scale(embedded) * modulation[0, 1] + modulation[0, 0]).astype(jnp.bfloat16)
    all_modulated = lax.all_gather(modulated, "pair", axis=0, tiled=True)
    local_cols = jnp.dot(all_modulated, w_qkv, preferred_element_type=jnp.float32).astype(
        jnp.bfloat16
    )
    projected = lax.all_to_all(local_cols, "pair", split_axis=0, concat_axis=1, tiled=True)
    head_width = projected.shape[1] // 3
    head_count = head_width // HDIM
    queries = projected[:, :head_width].reshape(tok_rows, head_count, HDIM)
    key_cols = projected[:, head_width : 2 * head_width]
    value_cols = projected[:, 2 * head_width :]
    score_scale = 1.0 / math.sqrt(HDIM)
    running_max = jnp.full((head_count, tok_rows), -1e30, jnp.float32)
    key_piece = lax.all_gather(key_cols, "ep", axis=0, tiled=True).reshape(-1, head_count, HDIM)
    value_piece = lax.all_gather(value_cols, "ep", axis=0, tiled=True).reshape(-1, head_count, HDIM)
    scores = (
        jnp.einsum("thd,nhd->htn", queries, key_piece, preferred_element_type=jnp.float32)
        * score_scale
    )
    new_max = jnp.maximum(running_max, jnp.max(scores, 2))
    weights = jnp.exp(scores - new_max[:, :, None])
    new_sum = jnp.sum(weights, 2)
    new_accum = jnp.einsum(
        "htn,nhd->htd", weights, value_piece.astype(jnp.float32), precision=lax.Precision.HIGHEST
    )
    attended = (
        (new_accum / new_sum[:, :, None])
        .transpose(1, 0, 2)
        .reshape(tok_rows, head_width)
        .astype(jnp.bfloat16)
    )
    return (own_next[None], attended[None])


Z_IN, X_IN, Y_IN, XY_IN, YX_IN, CORE_IN = 0, 1, 2, 3, 4, 5
CORE_OUT, XD_OUT, YD_OUT, X_OUT, Y_OUT, Z_OUT = 9, 10, 11, 12, 13, 14
KINDS = 15


def fused_kernel(
    hid_hbm,
    moe_gain_hbm,
    ids_hbm,
    gates_hbm,
    gate_hbm,
    up_hbm,
    down_hbm,
    final_gain_hbm,
    out_hbm,
    lat_hbm,
    in_hbm,
    mod_hbm,
    qkv_hbm,
    next_ref,
    att_ref,
    hid,
    moe_gain,
    ids,
    gates,
    final_gain,
    lat,
    rows,
    wg,
    wu,
    wd,
    wout,
    win,
    wqkv,
    act,
    sums,
    core_send,
    core_recv,
    diag_send,
    diag_recv,
    side_send,
    side_recv,
    z_send,
    z_recv,
    lats,
    mods,
    vels,
    cols,
    qkv,
    heads,
    whole,
    early_sem,
    load_sem,
    send_sem,
    recv_sem,
    small_send,
    small_recv,
    col_send,
    col_recv,
    head_send,
    head_recv,
):
    p, ep = lax.axis_index("pair"), lax.axis_index("ep")
    barrier = pltpu.get_barrier_semaphore()

    def greet(d, carry):
        other = lax.rem(p * 8 + ep + d, 32)
        pl.semaphore_signal(
            barrier,
            inc=1,
            device_id=(lax.div(other, 8), lax.rem(other, 8)),
            device_id_type=pl.DeviceIdType.MESH,
        )
        return carry

    early = [
        pltpu.make_async_copy(src, dst, early_sem.at[i])
        for i, (src, dst) in enumerate(
            (
                (hid_hbm, hid),
                (moe_gain_hbm, moe_gain),
                (ids_hbm, ids),
                (gates_hbm, gates),
                (final_gain_hbm, final_gain),
                (lat_hbm, lat),
                (mod_hbm.at[0], mods.at[0]),
            )
        )
    ]
    for load in early:
        load.start()
    lax.fori_loop(1, 32, greet, 0)
    x, y = lax.rem(p, 2), lax.div(p, 2)
    core, z = lax.rem(ep, 2), lax.div(ep, 2)
    px, py = y * 2 + (1 - x), (1 - y) * 2 + x
    pd = (1 - y) * 2 + (1 - x)
    pairs = (p, px, py, pd)
    core_ep = z * 2 + (1 - core)
    tok = hid.shape[1]
    half = tok // 2
    hidden_units = wg.shape[1]
    width = wd.shape[1]

    def place(k):
        low = lax.rem(lax.rem(z, 2) + lax.rem(k, 2), 2)
        high = lax.rem(lax.div(z, 2) + lax.div(k, 2), 2)
        return high * 2 + low

    def copy(src, dst, sent, received, device):
        return pltpu.make_async_remote_copy(
            src_ref=src,
            dst_ref=dst,
            send_sem=sent,
            recv_sem=received,
            device_id=device,
            device_id_type=pl.DeviceIdType.MESH,
        )

    top, low = pl.ds(0, half), pl.ds(half, half)

    def group(kind, k):
        if kind == Z_IN:
            src, dst, dev = rows.at[0, 0, 0], rows.at[k, 0, 0], (p, place(k) * 2 + core)
        elif kind == X_IN:
            src, dst, dev = rows.at[k, 0, 0], rows.at[k, 0, 1], (px, ep)
        elif kind == Y_IN:
            src, dst, dev = rows.at[k, 0, 0], rows.at[k, 0, 2], (py, ep)
        elif kind == XY_IN:
            src, dst, dev = rows.at[k, 0, 1, top], rows.at[k, 0, 3, top], (py, ep)
        elif kind == YX_IN:
            src, dst, dev = rows.at[k, 0, 2, low], rows.at[k, 0, 3, low], (px, ep)
        elif kind < CORE_OUT:
            r = kind - CORE_IN
            src, dst, dev = rows.at[k, 0, r], rows.at[k, 1, r], (p, core_ep)
        elif kind == CORE_OUT:
            src, dst, dev = core_send.at[k], core_recv.at[k], (p, core_ep)
        elif kind == XD_OUT:
            src, dst, dev = diag_send.at[k, 0], diag_recv.at[k, 0], (px, ep)
        elif kind == YD_OUT:
            src, dst, dev = diag_send.at[k, 1], diag_recv.at[k, 1], (py, ep)
        elif kind == X_OUT:
            src, dst, dev = side_send.at[k, 0], side_recv.at[k, 0], (px, ep)
        elif kind == Y_OUT:
            src, dst, dev = side_send.at[k, 1], side_recv.at[k, 1], (py, ep)
        else:
            src, dst, dev = z_send.at[k], z_recv.at[k], (p, place(k) * 2 + core)
        return copy(src, dst, send_sem.at[kind, k], recv_sem.at[kind, k], dev)

    loads = [
        pltpu.make_async_copy(src, dst, load_sem.at[i])
        for i, (src, dst) in enumerate(
            (
                (gate_hbm.at[0], wg),
                (up_hbm.at[0], wu),
                (down_hbm.at[0], wd),
                (out_hbm, wout),
                (in_hbm, win),
                (qkv_hbm, wqkv),
            )
        )
    ]

    for load in loads:
        load.start()
    for load in early:
        load.wait()
    rows[0, 0, 0] = (rms_scale(hid[0]) * moe_gain[...]).astype(jnp.bfloat16)
    lats[0] = jnp.zeros_like(lats[0])
    lats[0, :, : lat.shape[2]] = lat[0]
    pl.semaphore_wait(barrier, 31)

    def small(kind, r):
        buffer = (lats, mods, vels)[kind]
        return copy(
            buffer.at[0],
            buffer.at[r],
            small_send.at[kind, r],
            small_recv.at[kind, r],
            (pairs[r], ep),
        )

    def spread(k):
        @pl.when(k > 0)
        def _():
            group(Z_IN, k).wait_recv()

        group(X_IN, k).start()
        group(Y_IN, k).start()

        @pl.when(k == 0)
        def _():
            group(Z_IN, 1).start()
            group(Z_IN, 2).start()

        @pl.when(k == 1)
        def _():
            group(Z_IN, 3).start()

        group(CORE_IN, k).start()

    def forward(k):
        group(X_IN, k).wait_recv()
        group(XY_IN, k).start()
        group(CORE_IN + 1, k).start()
        group(Y_IN, k).wait_recv()
        group(YX_IN, k).start()
        group(CORE_IN + 2, k).start()

    def experts(k):
        group(XY_IN, k).wait_recv()
        group(YX_IN, k).wait_recv()
        group(CORE_IN + 3, k).start()
        for r in range(4):
            group(CORE_IN + r, k).wait_recv()

        @pl.when(k == 0)
        def _():
            for load in loads[:3]:
                load.wait()

        own = rows[k].reshape(8 * tok, width)
        step = min(256, hidden_units)
        for at in range(0, hidden_units, step):
            gated = jnp.dot(own, wg[:, at : at + step], preferred_element_type=jnp.float32)
            upward = jnp.dot(own, wu[:, at : at + step], preferred_element_type=jnp.float32)
            act[:, at : at + step] = (jax.nn.silu(gated) * upward).astype(jnp.bfloat16)
        step = min(512, width)
        for at in range(0, width, step):
            part = jnp.dot(act[...], wd[:, at : at + step], preferred_element_type=jnp.float32)
            part = part.reshape(2, 4, tok, step)
            sums[k, :, :, at : at + step] = part[0]
            core_send[k, :, :, at : at + step] = part[1].astype(jnp.bfloat16)
        group(CORE_OUT, k).start()

    def join_cores(k):
        group(CORE_OUT, k).wait_recv()
        diag = sums[k, 3] + core_recv[k, 3].astype(jnp.float32)
        diag_send[k] = diag.astype(jnp.bfloat16).reshape(2, half, width)
        group(XD_OUT, k).start()
        group(YD_OUT, k).start()
        for r in range(3):
            sums[k, r] = sums[k, r] + core_recv[k, r].astype(jnp.float32)

    def join_diagonal(k):
        group(XD_OUT, k).wait_recv()
        group(YD_OUT, k).wait_recv()
        side_send[k, 0, :half] = sums[k, 1, :half].astype(jnp.bfloat16)
        side_send[k, 0, half:] = (
            sums[k, 1, half:] + diag_recv[k, 1].astype(jnp.float32)
        ).astype(jnp.bfloat16)
        group(X_OUT, k).start()
        side_send[k, 1, :half] = (
            sums[k, 2, :half] + diag_recv[k, 0].astype(jnp.float32)
        ).astype(jnp.bfloat16)
        side_send[k, 1, half:] = sums[k, 2, half:].astype(jnp.bfloat16)
        group(Y_OUT, k).start()

    def join_sides(k):
        group(X_OUT, k).wait_recv()
        group(Y_OUT, k).wait_recv()
        total = (
            sums[k, 0]
            + side_recv[k, 0].astype(jnp.float32)
            + side_recv[k, 1].astype(jnp.float32)
        ).astype(jnp.bfloat16)

        @pl.when(k == 0)
        def _():
            z_recv[0] = total

        @pl.when(k > 0)
        def _():
            z_send[k] = total
            group(Z_OUT, k).start()

    stages = (
        (spread, 0),
        (forward, 1),
        (join_cores, 3),
        (join_sides, 4),
        (experts, 2),
        (join_diagonal, 3),
    )

    def turn(it, carry):
        for stage, lag in stages:

            @pl.when((it >= lag) & (it < lag + 4))
            def _(stage=stage, lag=lag):
                stage(it - lag)

        @pl.when(it == 0)
        def _():
            for r in range(1, 4):
                small(0, r).start()
                small(1, r).start()

        return carry

    lax.fori_loop(0, 8, turn, 0)

    mixed = jnp.zeros((tok, width), jnp.float32)
    eye = lax.broadcasted_iota(jnp.int32, (tok, tok), 0) == lax.broadcasted_iota(
        jnp.int32, (tok, tok), 1
    )
    for k in range(4):
        if k > 0:
            group(Z_OUT, k).wait_recv()
        weight = jnp.sum(jnp.where(ids[0] == place(k), gates[0], 0.0), 0, keepdims=True)
        weight = jnp.sum(jnp.where(eye, weight, 0.0), 1, keepdims=True)
        mixed = mixed + weight * z_recv[k].astype(jnp.float32)
    resid = hid[0] + mixed
    loads[3].wait()
    vels[0] = jnp.dot(
        (rms_scale(resid) * final_gain[...]).astype(jnp.bfloat16),
        wout[...],
        preferred_element_type=jnp.float32,
    )
    for r in range(1, 4):
        small(2, r).start()
    for kind in range(3):
        for r in range(1, 4):
            small(kind, r).wait_recv()

    is_cond = x == 0
    half_channels = lat.shape[2]

    def advance(first, second):
        cond_vel = jnp.where(is_cond, vels[first], vels[second])
        uncond_vel = jnp.where(is_cond, vels[second], vels[first])
        cond_lat = jnp.where(is_cond, lats[first], lats[second])[:, :half_channels]
        uncond_lat = jnp.where(is_cond, lats[second], lats[first])[:, :half_channels]
        guided = uncond_vel + GUIDANCE * (cond_vel - uncond_vel)
        return jnp.concatenate([cond_lat, uncond_lat], 1) + STEP_SIZE * guided

    advanced = advance(0, 1)
    next_ref[0] = jnp.where(is_cond, advanced[:, :half_channels], advanced[:, half_channels:])
    both = jnp.concatenate([advanced, advance(2, 3)], 0).astype(jnp.bfloat16)
    loads[4].wait()
    scaled = rms_scale(jnp.dot(both, win[...], preferred_element_type=jnp.float32))
    modulated = jnp.concatenate(
        [
            (scaled[(r // 2) * tok : (r // 2 + 1) * tok] * mods[r, 1:2] + mods[r, 0:1]).astype(
                jnp.bfloat16
            )
            for r in range(4)
        ],
        0,
    )
    loads[5].wait()
    local = jnp.dot(modulated, wqkv[...], preferred_element_type=jnp.float32).astype(jnp.bfloat16)
    blocks = local.shape[1] // HDIM
    for r in range(4):
        for b in range(blocks):
            cols[r, b] = local[r * tok : (r + 1) * tok, b * HDIM : (b + 1) * HDIM]

    def column(r, b):
        number = p * blocks + b
        sort, head = lax.div(number, 8), lax.rem(number, 8)
        return head, sort, copy(
            cols.at[r, b],
            qkv.at[sort, ep],
            col_send.at[r, b],
            col_recv.at[sort, ep],
            (pairs[r], head),
        )

    def each_column(act_on, keep):
        for r in (3, 1, 2, 0):
            for b in range(blocks):
                head, sort, moved = column(r, b)
                if r > 0:
                    act_on(moved)
                    continue

                @pl.when(head != ep)
                def _(moved=moved):
                    act_on(moved)

                if keep:

                    @pl.when(head == ep)
                    def _(sort=sort, b=b):
                        qkv[sort, ep] = cols[0, b]

    each_column(lambda moved: moved.start(), True)
    for sort in range(3):
        for j in range(8):

            @pl.when((lax.div(sort * 8 + ep, blocks) != p) | (ep != j))
            def _(sort=sort, j=j):
                copy(
                    qkv.at[sort, j],
                    qkv.at[sort, j],
                    col_send.at[0, 0],
                    col_recv.at[sort, j],
                    (px, ep),
                ).wait_recv()

    query, key, value = (qkv[sort].reshape(8 * tok, HDIM) for sort in range(3))
    scores = lax.dot_general(
        query, key, (((1,), (1,)), ((), ())), preferred_element_type=jnp.float32
    ) * (1.0 / math.sqrt(HDIM))
    weights = jnp.exp(scores - jnp.max(scores, 1, keepdims=True))
    total = jnp.sum(weights, 1, keepdims=True)
    mixed_values = jnp.dot(
        weights.astype(jnp.bfloat16), value, preferred_element_type=jnp.float32
    )
    heads[...] = (mixed_values / total).astype(jnp.bfloat16).reshape(8, tok, HDIM)

    def result(d):
        j = lax.rem(ep + d, 8)
        return copy(heads.at[j], whole.at[ep], head_send.at[d], head_recv.at[d], (p, j))

    for d in range(1, 8):
        result(d).start()
    whole[ep] = heads[ep]
    for d in range(1, 8):
        j = lax.rem(ep + 8 - d, 8)
        copy(whole.at[j], whole.at[j], head_send.at[d], head_recv.at[d], (px, ep)).wait_recv()
    for h in range(8):
        att_ref[0, :, h * HDIM : (h + 1) * HDIM] = whole[h]

    def settle(k, carry):
        for kind in range(KINDS):
            if kind in (Z_IN, Z_OUT):

                @pl.when(k > 0)
                def _(kind=kind):
                    group(kind, k).wait_send()

            else:
                group(kind, k).wait_send()
        return carry

    lax.fori_loop(0, 4, settle, 0)
    for kind in range(3):
        for r in range(1, 4):
            small(kind, r).wait_send()
    each_column(lambda moved: moved.wait_send(), False)
    for d in range(1, 8):
        result(d).wait_send()


def fused(
    hidden,
    moe_gain,
    expert_ids,
    gate_weights,
    w_gate,
    w_up,
    w_down,
    final_gain,
    w_out,
    latent,
    w_in,
    modulation,
    w_qkv,
):
    tok, width = hidden.shape[1:]
    units = w_gate.shape[2]
    channels = w_out.shape[1]
    columns = w_qkv.shape[1]
    blocks = columns // HDIM
    b16, f32 = jnp.bfloat16, jnp.float32
    vmem, hbm = pl.BlockSpec(memory_space=pltpu.VMEM), pl.BlockSpec(memory_space=pl.ANY)
    dma = pltpu.SemaphoreType.DMA
    half = tok // 2
    return pl.pallas_call(
        fused_kernel,
        out_shape=(
            jax.ShapeDtypeStruct(latent.shape, f32),
            jax.ShapeDtypeStruct((1, tok, 8 * HDIM), b16),
        ),
        in_specs=[hbm] * 13,
        out_specs=(vmem, vmem),
        scratch_shapes=[
            pltpu.VMEM(hidden.shape, f32),
            pltpu.VMEM((1, width), f32),
            pltpu.VMEM((1, 2, tok), jnp.int32),
            pltpu.VMEM((1, 2, tok), f32),
            pltpu.VMEM((1, width), f32),
            pltpu.VMEM(latent.shape, f32),
            pltpu.VMEM((4, 2, 4, tok, width), b16),
            pltpu.VMEM((width, units), b16),
            pltpu.VMEM((width, units), b16),
            pltpu.VMEM((units, width), b16),
            pltpu.VMEM(w_out.shape, b16),
            pltpu.VMEM(w_in.shape, b16),
            pltpu.VMEM(w_qkv.shape, b16),
            pltpu.VMEM((8 * tok, units), b16),
            pltpu.VMEM((4, 4, tok, width), f32),
            pltpu.VMEM((4, 4, tok, width), b16),
            pltpu.VMEM((4, 4, tok, width), b16),
            pltpu.VMEM((4, 2, half, width), b16),
            pltpu.VMEM((4, 2, half, width), b16),
            pltpu.VMEM((4, 2, tok, width), b16),
            pltpu.VMEM((4, 2, tok, width), b16),
            pltpu.VMEM((4, tok, width), b16),
            pltpu.VMEM((4, tok, width), b16),
            pltpu.VMEM((4, tok, channels), f32),
            pltpu.VMEM((4, 2, width), f32),
            pltpu.VMEM((4, tok, channels), f32),
            pltpu.VMEM((4, blocks, tok, HDIM), b16),
            pltpu.VMEM((3, 8, tok, HDIM), b16),
            pltpu.VMEM((8, tok, HDIM), b16),
            pltpu.VMEM((8, tok, HDIM), b16),
            dma((7,)),
            dma((6,)),
            dma((KINDS, 4)),
            dma((KINDS, 4)),
            dma((3, 4)),
            dma((3, 4)),
            dma((4, blocks)),
            dma((3, 8)),
            dma((8,)),
            dma((8,)),
        ],
        compiler_params=pltpu.CompilerParams(
            collective_id=0, has_side_effects=True, vmem_limit_bytes=60 * 2**20
        ),
        name="guided_step",
    )(
        hidden,
        moe_gain[None],
        expert_ids.transpose(0, 2, 1),
        gate_weights.transpose(0, 2, 1),
        w_gate,
        w_up,
        w_down,
        final_gain[None],
        w_out,
        latent,
        w_in,
        modulation,
        w_qkv,
    )


def choose(mesh):
    if mesh.shape["pair"] == 4 and mesh.shape["ep"] == 8:
        return fused
    return per_device


def solution(mesh):
    return jax.shard_map(
        choose(mesh),
        mesh=mesh,
        in_specs=(
            P("pair", "ep", None),
            P(),
            P("pair", "ep", None),
            P("pair", "ep", None),
            P("ep", None, "pair"),
            P("ep", None, "pair"),
            P("ep", "pair", None),
            P(),
            P(),
            P("pair", "ep", None),
            P(),
            P("pair", None, None),
            P(None, "pair"),
        ),
        out_specs=(P("pair", "ep", None), P("pair", "ep", None)),
        check_vma=False,
    )
```

```python
import math

import jax
import jax.numpy as jnp
from jax import lax
from jax.experimental import pallas as pl
from jax.experimental.pallas import tpu as pltpu
from jax.sharding import PartitionSpec as P

HDIM = 128


EPSILON = 1e-06
GUIDANCE = 3.0
STEP_SIZE = 0.25


def from_partner(value, axis, bit):
    mask = 2**bit
    pairs = [(source, source ^ mask) for source in range(lax.axis_size(axis))]
    return lax.ppermute(value, axis, pairs)


def rms_scale(values):
    return values * lax.rsqrt(jnp.mean(values * values, -1, keepdims=True) + EPSILON)


def per_device(
    hidden,
    moe_gain,
    expert_ids,
    gate_weights,
    w_gate,
    w_up,
    w_down,
    final_gain,
    w_out,
    latent,
    w_in,
    modulation,
    w_qkv,
):
    tok_rows = hidden.shape[1]
    model_width = hidden.shape[2]
    experts = lax.axis_size("ep") // 2
    capacity = 4 * tok_rows // experts
    slot_count = experts * capacity
    own_hidden = hidden[0]
    normed = (rms_scale(own_hidden) * moe_gain).astype(jnp.bfloat16)
    flat_ids = expert_ids[0].reshape(-1)
    onehot = (flat_ids[:, None] == jnp.arange(experts, dtype=jnp.int32)[None, :]).astype(jnp.int32)
    slot_rank = jnp.sum((jnp.cumsum(onehot, 0) - onehot) * onehot, 1)
    places = flat_ids * capacity + slot_rank
    matches = places[None, :] == jnp.arange(slot_count, dtype=jnp.int32)[:, None]
    dispatch_mat = jnp.sum(matches.reshape(slot_count, tok_rows, 2).astype(jnp.float32), 2).astype(
        jnp.bfloat16
    )
    buffers = jnp.dot(dispatch_mat, normed, preferred_element_type=jnp.float32).astype(jnp.bfloat16)
    doubled = jnp.broadcast_to(
        buffers.reshape(experts, 1, capacity, model_width), (experts, 2, capacity, model_width)
    ).reshape(2 * experts, capacity, model_width)
    arrived = lax.all_to_all(doubled, "ep", split_axis=0, concat_axis=0, tiled=True)
    all_rows = lax.all_gather(arrived.reshape(-1, model_width), "pair", axis=0, tiled=True)
    gate_mat = w_gate[0]
    up_mat = w_up[0]
    down_mat = w_down[0]
    gated = jnp.dot(all_rows, gate_mat, preferred_element_type=jnp.float32)
    upward = jnp.dot(all_rows, up_mat, preferred_element_type=jnp.float32)
    active = (jax.nn.silu(gated) * upward).astype(jnp.bfloat16)
    halves = lax.psum_scatter(
        jnp.dot(active, down_mat, preferred_element_type=jnp.float32).astype(jnp.bfloat16),
        "pair",
        scatter_dimension=0,
        tiled=True,
    )
    returned = lax.all_to_all(
        halves.reshape(2 * experts, capacity, model_width),
        "ep",
        split_axis=0,
        concat_axis=0,
        tiled=True,
    )
    paired = returned.reshape(experts, 2, capacity, model_width)
    summed = (paired[:, 0].astype(jnp.float32) + paired[:, 1].astype(jnp.float32)).reshape(
        slot_count, model_width
    )
    combine_mat = jnp.sum(
        jnp.where(matches, gate_weights[0].reshape(-1)[None, :], 0.0).reshape(
            slot_count, tok_rows, 2
        ),
        2,
    )
    mixed_out = jnp.einsum("st,sd->td", combine_mat, summed, precision=lax.Precision.HIGHEST)
    resid = own_hidden + mixed_out
    velocity = jnp.dot(
        (rms_scale(resid) * final_gain).astype(jnp.bfloat16),
        w_out,
        preferred_element_type=jnp.float32,
    )
    own_latent = latent[0]
    outgoing = jnp.concatenate([velocity, own_latent], 1)
    incoming = from_partner(outgoing, "pair", 0)
    channels = velocity.shape[1]
    partner_vel = incoming[:, :channels]
    partner_latent = incoming[:, channels:]
    is_cond = lax.axis_index("pair") % 2 == 0
    cond_vel = jnp.where(is_cond, velocity, partner_vel)
    uncond_vel = jnp.where(is_cond, partner_vel, velocity)
    guided = uncond_vel + GUIDANCE * (cond_vel - uncond_vel)
    whole_latent = jnp.where(
        is_cond,
        jnp.concatenate([own_latent, partner_latent], 1),
        jnp.concatenate([partner_latent, own_latent], 1),
    )
    advanced = whole_latent + STEP_SIZE * guided
    half_width = own_latent.shape[1]
    own_next = jnp.where(is_cond, advanced[:, :half_width], advanced[:, half_width:])
    embedded = jnp.dot(advanced.astype(jnp.bfloat16), w_in, preferred_element_type=jnp.float32)
    modulated = (rms_scale(embedded) * modulation[0, 1] + modulation[0, 0]).astype(jnp.bfloat16)
    all_modulated = lax.all_gather(modulated, "pair", axis=0, tiled=True)
    local_cols = jnp.dot(all_modulated, w_qkv, preferred_element_type=jnp.float32).astype(
        jnp.bfloat16
    )
    projected = lax.all_to_all(local_cols, "pair", split_axis=0, concat_axis=1, tiled=True)
    head_width = projected.shape[1] // 3
    head_count = head_width // HDIM
    queries = projected[:, :head_width].reshape(tok_rows, head_count, HDIM)
    key_cols = projected[:, head_width : 2 * head_width]
    value_cols = projected[:, 2 * head_width :]
    score_scale = 1.0 / math.sqrt(HDIM)
    running_max = jnp.full((head_count, tok_rows), -1e30, jnp.float32)
    key_piece = lax.all_gather(key_cols, "ep", axis=0, tiled=True).reshape(-1, head_count, HDIM)
    value_piece = lax.all_gather(value_cols, "ep", axis=0, tiled=True).reshape(-1, head_count, HDIM)
    scores = (
        jnp.einsum("thd,nhd->htn", queries, key_piece, preferred_element_type=jnp.float32)
        * score_scale
    )
    new_max = jnp.maximum(running_max, jnp.max(scores, 2))
    weights = jnp.exp(scores - new_max[:, :, None])
    new_sum = jnp.sum(weights, 2)
    new_accum = jnp.einsum(
        "htn,nhd->htd", weights, value_piece.astype(jnp.float32), precision=lax.Precision.HIGHEST
    )
    attended = (
        (new_accum / new_sum[:, :, None])
        .transpose(1, 0, 2)
        .reshape(tok_rows, head_width)
        .astype(jnp.bfloat16)
    )
    return (own_next[None], attended[None])


Z_IN, X_IN, Y_IN, XY_IN, YX_IN, CORE_IN = 0, 1, 2, 3, 4, 5
CORE_OUT, XD_OUT, YD_OUT, X_OUT, Y_OUT, Z_OUT = 9, 10, 11, 12, 13, 14
KINDS = 15


def fused_kernel(
    hid_hbm,
    moe_gain_hbm,
    ids_hbm,
    gates_hbm,
    gate_hbm,
    up_hbm,
    down_hbm,
    final_gain_hbm,
    out_hbm,
    lat_hbm,
    in_hbm,
    mod_hbm,
    qkv_hbm,
    next_ref,
    att_ref,
    hid,
    moe_gain,
    ids,
    gates,
    final_gain,
    lat,
    rows,
    wg,
    wu,
    wd,
    wout,
    win,
    wqkv,
    act,
    sums,
    core_send,
    core_recv,
    diag_send,
    diag_recv,
    side_send,
    side_recv,
    z_send,
    z_recv,
    lats,
    mods,
    vels,
    cols,
    qkv,
    heads,
    whole,
    early_sem,
    load_sem,
    send_sem,
    recv_sem,
    small_send,
    small_recv,
    col_send,
    col_recv,
    head_send,
    head_recv,
):
    p, ep = lax.axis_index("pair"), lax.axis_index("ep")
    barrier = pltpu.get_barrier_semaphore()

    def greet(d, carry):
        other = lax.rem(p * 8 + ep + d, 32)
        pl.semaphore_signal(
            barrier,
            inc=1,
            device_id=(lax.div(other, 8), lax.rem(other, 8)),
            device_id_type=pl.DeviceIdType.MESH,
        )
        return carry

    early = [
        pltpu.make_async_copy(src, dst, early_sem.at[i])
        for i, (src, dst) in enumerate(
            (
                (hid_hbm, hid),
                (moe_gain_hbm, moe_gain),
                (ids_hbm, ids),
                (gates_hbm, gates),
                (final_gain_hbm, final_gain),
                (lat_hbm, lat),
                (mod_hbm.at[0], mods.at[0]),
            )
        )
    ]
    for load in early:
        load.start()
    lax.fori_loop(1, 32, greet, 0)
    x, y = lax.rem(p, 2), lax.div(p, 2)
    core, z = lax.rem(ep, 2), lax.div(ep, 2)
    px, py = y * 2 + (1 - x), (1 - y) * 2 + x
    pd = (1 - y) * 2 + (1 - x)
    pairs = (p, px, py, pd)
    core_ep = z * 2 + (1 - core)
    tok = hid.shape[1]
    half = tok // 2
    hidden_units = wg.shape[1]
    width = wd.shape[1]

    def place(k):
        low = lax.rem(lax.rem(z, 2) + lax.rem(k, 2), 2)
        high = lax.rem(lax.div(z, 2) + lax.div(k, 2), 2)
        return high * 2 + low

    def copy(src, dst, sent, received, device):
        return pltpu.make_async_remote_copy(
            src_ref=src,
            dst_ref=dst,
            send_sem=sent,
            recv_sem=received,
            device_id=device,
            device_id_type=pl.DeviceIdType.MESH,
        )

    top, low = pl.ds(0, half), pl.ds(half, half)

    def group(kind, k):
        if kind == Z_IN:
            src, dst, dev = rows.at[0, 0, 0], rows.at[k, 0, 0], (p, place(k) * 2 + core)
        elif kind == X_IN:
            src, dst, dev = rows.at[k, 0, 0], rows.at[k, 0, 1], (px, ep)
        elif kind == Y_IN:
            src, dst, dev = rows.at[k, 0, 0], rows.at[k, 0, 2], (py, ep)
        elif kind == XY_IN:
            src, dst, dev = rows.at[k, 0, 1, top], rows.at[k, 0, 3, top], (py, ep)
        elif kind == YX_IN:
            src, dst, dev = rows.at[k, 0, 2, low], rows.at[k, 0, 3, low], (px, ep)
        elif kind < CORE_OUT:
            r = kind - CORE_IN
            src, dst, dev = rows.at[k, 0, r], rows.at[k, 1, r], (p, core_ep)
        elif kind == CORE_OUT:
            src, dst, dev = core_send.at[k], core_recv.at[k], (p, core_ep)
        elif kind == XD_OUT:
            src, dst, dev = diag_send.at[k, 0], diag_recv.at[k, 0], (px, ep)
        elif kind == YD_OUT:
            src, dst, dev = diag_send.at[k, 1], diag_recv.at[k, 1], (py, ep)
        elif kind == X_OUT:
            src, dst, dev = side_send.at[k, 0], side_recv.at[k, 0], (px, ep)
        elif kind == Y_OUT:
            src, dst, dev = side_send.at[k, 1], side_recv.at[k, 1], (py, ep)
        else:
            src, dst, dev = z_send.at[k], z_recv.at[k], (p, place(k) * 2 + core)
        return copy(src, dst, send_sem.at[kind, k], recv_sem.at[kind, k], dev)

    loads = [
        pltpu.make_async_copy(src, dst, load_sem.at[i])
        for i, (src, dst) in enumerate(
            (
                (gate_hbm.at[0], wg),
                (up_hbm.at[0], wu),
                (down_hbm.at[0], wd),
                (out_hbm, wout),
                (in_hbm, win),
                (qkv_hbm, wqkv),
            )
        )
    ]

    for load in loads:
        load.start()
    for load in early:
        load.wait()
    rows[0, 0, 0] = (rms_scale(hid[0]) * moe_gain[...]).astype(jnp.bfloat16)
    lats[0] = jnp.zeros_like(lats[0])
    lats[0, :, : lat.shape[2]] = lat[0]
    pl.semaphore_wait(barrier, 31)

    def small(kind, r):
        buffer = (lats, mods, vels)[kind]
        return copy(
            buffer.at[0],
            buffer.at[r],
            small_send.at[kind, r],
            small_recv.at[kind, r],
            (pairs[r], ep),
        )

    def spread(k):
        @pl.when(k > 0)
        def _():
            group(Z_IN, k).wait_recv()

        group(X_IN, k).start()
        group(Y_IN, k).start()

        @pl.when(k == 0)
        def _():
            group(Z_IN, 1).start()
            group(Z_IN, 2).start()

        group(CORE_IN, k).start()

    def forward(k):
        group(X_IN, k).wait_recv()
        group(XY_IN, k).start()
        group(CORE_IN + 1, k).start()
        group(Y_IN, k).wait_recv()
        group(YX_IN, k).start()
        group(CORE_IN + 2, k).start()

    def experts(k):
        group(XY_IN, k).wait_recv()
        group(YX_IN, k).wait_recv()
        group(CORE_IN + 3, k).start()
        for r in range(4):
            group(CORE_IN + r, k).wait_recv()

        @pl.when(k == 0)
        def _():
            for load in loads[:3]:
                load.wait()

        own = rows[k].reshape(8 * tok, width)
        step = min(256, hidden_units)
        for at in range(0, hidden_units, step):
            gated = jnp.dot(own, wg[:, at : at + step], preferred_element_type=jnp.float32)
            upward = jnp.dot(own, wu[:, at : at + step], preferred_element_type=jnp.float32)
            act[:, at : at + step] = (jax.nn.silu(gated) * upward).astype(jnp.bfloat16)
        step = min(512, width)
        for at in range(0, width, step):
            part = jnp.dot(act[...], wd[:, at : at + step], preferred_element_type=jnp.float32)
            part = part.reshape(2, 4, tok, step)
            sums[k, :, :, at : at + step] = part[0]
            core_send[k, :, :, at : at + step] = part[1].astype(jnp.bfloat16)
        group(CORE_OUT, k).start()

    def join_cores(k):
        group(CORE_OUT, k).wait_recv()
        diag = sums[k, 3] + core_recv[k, 3].astype(jnp.float32)
        diag_send[k] = diag.astype(jnp.bfloat16).reshape(2, half, width)
        group(XD_OUT, k).start()
        group(YD_OUT, k).start()
        for r in range(3):
            sums[k, r] = sums[k, r] + core_recv[k, r].astype(jnp.float32)

    def join_diagonal(k):
        group(XD_OUT, k).wait_recv()
        group(YD_OUT, k).wait_recv()
        side_send[k, 0, :half] = sums[k, 1, :half].astype(jnp.bfloat16)
        side_send[k, 0, half:] = (
            sums[k, 1, half:] + diag_recv[k, 1].astype(jnp.float32)
        ).astype(jnp.bfloat16)
        group(X_OUT, k).start()
        side_send[k, 1, :half] = (
            sums[k, 2, :half] + diag_recv[k, 0].astype(jnp.float32)
        ).astype(jnp.bfloat16)
        side_send[k, 1, half:] = sums[k, 2, half:].astype(jnp.bfloat16)
        group(Y_OUT, k).start()

    def join_sides(k):
        group(X_OUT, k).wait_recv()
        group(Y_OUT, k).wait_recv()
        total = (
            sums[k, 0]
            + side_recv[k, 0].astype(jnp.float32)
            + side_recv[k, 1].astype(jnp.float32)
        ).astype(jnp.bfloat16)

        @pl.when(k == 0)
        def _():
            z_recv[0] = total

        @pl.when(k > 0)
        def _():
            z_send[k] = total
            group(Z_OUT, k).start()

    spread(0)
    for r in range(1, 4):
        small(0, r).start()
        small(1, r).start()
    forward(0)
    group(Z_IN, 3).start()
    spread(1)
    spread(2)

    def turn(k, carry):
        @pl.when(k == 1)
        def _():
            forward(1)
            spread(3)
            forward(2)

        @pl.when(k == 2)
        def _():
            forward(3)

        @pl.when(k >= 1)
        def _():
            join_cores(k - 1)

        experts(k)

        @pl.when(k >= 2)
        def _():
            join_sides(k - 2)

        @pl.when(k >= 1)
        def _():
            join_diagonal(k - 1)

        return carry

    lax.fori_loop(0, 4, turn, 0)
    join_cores(3)
    join_sides(2)
    join_diagonal(3)
    join_sides(3)

    mixed = jnp.zeros((tok, width), jnp.float32)
    eye = lax.broadcasted_iota(jnp.int32, (tok, tok), 0) == lax.broadcasted_iota(
        jnp.int32, (tok, tok), 1
    )
    for k in range(4):
        if k > 0:
            group(Z_OUT, k).wait_recv()
        weight = jnp.sum(jnp.where(ids[0] == place(k), gates[0], 0.0), 0, keepdims=True)
        weight = jnp.sum(jnp.where(eye, weight, 0.0), 1, keepdims=True)
        mixed = mixed + weight * z_recv[k].astype(jnp.float32)
    resid = hid[0] + mixed
    loads[3].wait()
    vels[0] = jnp.dot(
        (rms_scale(resid) * final_gain[...]).astype(jnp.bfloat16),
        wout[...],
        preferred_element_type=jnp.float32,
    )
    for r in range(1, 4):
        small(2, r).start()
    for kind in range(3):
        for r in range(1, 4):
            small(kind, r).wait_recv()

    is_cond = x == 0
    half_channels = lat.shape[2]

    def advance(first, second):
        cond_vel = jnp.where(is_cond, vels[first], vels[second])
        uncond_vel = jnp.where(is_cond, vels[second], vels[first])
        cond_lat = jnp.where(is_cond, lats[first], lats[second])[:, :half_channels]
        uncond_lat = jnp.where(is_cond, lats[second], lats[first])[:, :half_channels]
        guided = uncond_vel + GUIDANCE * (cond_vel - uncond_vel)
        return jnp.concatenate([cond_lat, uncond_lat], 1) + STEP_SIZE * guided

    advanced = advance(0, 1)
    next_ref[0] = jnp.where(is_cond, advanced[:, :half_channels], advanced[:, half_channels:])
    both = jnp.concatenate([advanced, advance(2, 3)], 0).astype(jnp.bfloat16)
    loads[4].wait()
    scaled = rms_scale(jnp.dot(both, win[...], preferred_element_type=jnp.float32))
    modulated = jnp.concatenate(
        [
            (scaled[(r // 2) * tok : (r // 2 + 1) * tok] * mods[r, 1:2] + mods[r, 0:1]).astype(
                jnp.bfloat16
            )
            for r in range(4)
        ],
        0,
    )
    loads[5].wait()
    local = jnp.dot(modulated, wqkv[...], preferred_element_type=jnp.float32).astype(jnp.bfloat16)
    blocks = local.shape[1] // HDIM
    for r in range(4):
        for b in range(blocks):
            cols[r, b] = local[r * tok : (r + 1) * tok, b * HDIM : (b + 1) * HDIM]

    def column(r, b):
        number = p * blocks + b
        sort, head = lax.div(number, 8), lax.rem(number, 8)
        return head, sort, copy(
            cols.at[r, b],
            qkv.at[sort, ep],
            col_send.at[r, b],
            col_recv.at[sort, ep],
            (pairs[r], head),
        )

    def each_column(act_on, keep):
        for r in (3, 1, 2, 0):
            for b in range(blocks):
                head, sort, moved = column(r, b)
                if r > 0:
                    act_on(moved)
                    continue

                @pl.when(head != ep)
                def _(moved=moved):
                    act_on(moved)

                if keep:

                    @pl.when(head == ep)
                    def _(sort=sort, b=b):
                        qkv[sort, ep] = cols[0, b]

    each_column(lambda moved: moved.start(), True)
    for sort in range(3):
        for j in range(8):

            @pl.when((lax.div(sort * 8 + ep, blocks) != p) | (ep != j))
            def _(sort=sort, j=j):
                copy(
                    qkv.at[sort, j],
                    qkv.at[sort, j],
                    col_send.at[0, 0],
                    col_recv.at[sort, j],
                    (px, ep),
                ).wait_recv()

    query, key, value = (qkv[sort].reshape(8 * tok, HDIM) for sort in range(3))
    scores = lax.dot_general(
        query, key, (((1,), (1,)), ((), ())), preferred_element_type=jnp.float32
    ) * (1.0 / math.sqrt(HDIM))
    weights = jnp.exp(scores - jnp.max(scores, 1, keepdims=True))
    total = jnp.sum(weights, 1, keepdims=True)
    mixed_values = jnp.dot(
        weights.astype(jnp.bfloat16), value, preferred_element_type=jnp.float32
    )
    heads[...] = (mixed_values / total).astype(jnp.bfloat16).reshape(8, tok, HDIM)

    def result(d):
        j = lax.rem(ep + d, 8)
        return copy(heads.at[j], whole.at[ep], head_send.at[d], head_recv.at[d], (p, j))

    for d in range(1, 8):
        result(d).start()
    whole[ep] = heads[ep]
    for d in range(1, 8):
        j = lax.rem(ep + 8 - d, 8)
        copy(whole.at[j], whole.at[j], head_send.at[d], head_recv.at[d], (px, ep)).wait_recv()
    for h in range(8):
        att_ref[0, :, h * HDIM : (h + 1) * HDIM] = whole[h]

    def settle(k, carry):
        for kind in range(KINDS):
            if kind in (Z_IN, Z_OUT):

                @pl.when(k > 0)
                def _(kind=kind):
                    group(kind, k).wait_send()

            else:
                group(kind, k).wait_send()
        return carry

    lax.fori_loop(0, 4, settle, 0)
    for kind in range(3):
        for r in range(1, 4):
            small(kind, r).wait_send()
    each_column(lambda moved: moved.wait_send(), False)
    for d in range(1, 8):
        result(d).wait_send()


def fused(
    hidden,
    moe_gain,
    expert_ids,
    gate_weights,
    w_gate,
    w_up,
    w_down,
    final_gain,
    w_out,
    latent,
    w_in,
    modulation,
    w_qkv,
):
    tok, width = hidden.shape[1:]
    units = w_gate.shape[2]
    channels = w_out.shape[1]
    columns = w_qkv.shape[1]
    blocks = columns // HDIM
    b16, f32 = jnp.bfloat16, jnp.float32
    vmem, hbm = pl.BlockSpec(memory_space=pltpu.VMEM), pl.BlockSpec(memory_space=pl.ANY)
    dma = pltpu.SemaphoreType.DMA
    half = tok // 2
    return pl.pallas_call(
        fused_kernel,
        out_shape=(
            jax.ShapeDtypeStruct(latent.shape, f32),
            jax.ShapeDtypeStruct((1, tok, 8 * HDIM), b16),
        ),
        in_specs=[hbm] * 13,
        out_specs=(vmem, vmem),
        scratch_shapes=[
            pltpu.VMEM(hidden.shape, f32),
            pltpu.VMEM((1, width), f32),
            pltpu.VMEM((1, 2, tok), jnp.int32),
            pltpu.VMEM((1, 2, tok), f32),
            pltpu.VMEM((1, width), f32),
            pltpu.VMEM(latent.shape, f32),
            pltpu.VMEM((4, 2, 4, tok, width), b16),
            pltpu.VMEM((width, units), b16),
            pltpu.VMEM((width, units), b16),
            pltpu.VMEM((units, width), b16),
            pltpu.VMEM(w_out.shape, b16),
            pltpu.VMEM(w_in.shape, b16),
            pltpu.VMEM(w_qkv.shape, b16),
            pltpu.VMEM((8 * tok, units), b16),
            pltpu.VMEM((4, 4, tok, width), f32),
            pltpu.VMEM((4, 4, tok, width), b16),
            pltpu.VMEM((4, 4, tok, width), b16),
            pltpu.VMEM((4, 2, half, width), b16),
            pltpu.VMEM((4, 2, half, width), b16),
            pltpu.VMEM((4, 2, tok, width), b16),
            pltpu.VMEM((4, 2, tok, width), b16),
            pltpu.VMEM((4, tok, width), b16),
            pltpu.VMEM((4, tok, width), b16),
            pltpu.VMEM((4, tok, channels), f32),
            pltpu.VMEM((4, 2, width), f32),
            pltpu.VMEM((4, tok, channels), f32),
            pltpu.VMEM((4, blocks, tok, HDIM), b16),
            pltpu.VMEM((3, 8, tok, HDIM), b16),
            pltpu.VMEM((8, tok, HDIM), b16),
            pltpu.VMEM((8, tok, HDIM), b16),
            dma((7,)),
            dma((6,)),
            dma((KINDS, 4)),
            dma((KINDS, 4)),
            dma((3, 4)),
            dma((3, 4)),
            dma((4, blocks)),
            dma((3, 8)),
            dma((8,)),
            dma((8,)),
        ],
        compiler_params=pltpu.CompilerParams(
            collective_id=0, has_side_effects=True, vmem_limit_bytes=60 * 2**20
        ),
        name="guided_step",
    )(
        hidden,
        moe_gain[None],
        expert_ids.transpose(0, 2, 1),
        gate_weights.transpose(0, 2, 1),
        w_gate,
        w_up,
        w_down,
        final_gain[None],
        w_out,
        latent,
        w_in,
        modulation,
        w_qkv,
    )


def choose(mesh):
    if mesh.shape["pair"] == 4 and mesh.shape["ep"] == 8:
        return fused
    return per_device


def solution(mesh):
    return jax.shard_map(
        choose(mesh),
        mesh=mesh,
        in_specs=(
            P("pair", "ep", None),
            P(),
            P("pair", "ep", None),
            P("pair", "ep", None),
            P("ep", None, "pair"),
            P("ep", None, "pair"),
            P("ep", "pair", None),
            P(),
            P(),
            P("pair", "ep", None),
            P(),
            P("pair", None, None),
            P(None, "pair"),
        ),
        out_specs=(P("pair", "ep", None), P("pair", "ep", None)),
        check_vma=False,
    )
```

```python
import math

import jax
import jax.numpy as jnp
from jax import lax
from jax.experimental import pallas as pl
from jax.experimental.pallas import tpu as pltpu
from jax.sharding import PartitionSpec as P

HDIM = 128


EPSILON = 1e-06
GUIDANCE = 3.0
STEP_SIZE = 0.25


def from_partner(value, axis, bit):
    mask = 2**bit
    pairs = [(source, source ^ mask) for source in range(lax.axis_size(axis))]
    return lax.ppermute(value, axis, pairs)


def rms_scale(values):
    return values * lax.rsqrt(jnp.mean(values * values, -1, keepdims=True) + EPSILON)


def per_device(
    hidden,
    moe_gain,
    expert_ids,
    gate_weights,
    w_gate,
    w_up,
    w_down,
    final_gain,
    w_out,
    latent,
    w_in,
    modulation,
    w_qkv,
):
    tok_rows = hidden.shape[1]
    model_width = hidden.shape[2]
    experts = lax.axis_size("ep") // 2
    capacity = 4 * tok_rows // experts
    slot_count = experts * capacity
    own_hidden = hidden[0]
    normed = (rms_scale(own_hidden) * moe_gain).astype(jnp.bfloat16)
    flat_ids = expert_ids[0].reshape(-1)
    onehot = (flat_ids[:, None] == jnp.arange(experts, dtype=jnp.int32)[None, :]).astype(jnp.int32)
    slot_rank = jnp.sum((jnp.cumsum(onehot, 0) - onehot) * onehot, 1)
    places = flat_ids * capacity + slot_rank
    matches = places[None, :] == jnp.arange(slot_count, dtype=jnp.int32)[:, None]
    dispatch_mat = jnp.sum(matches.reshape(slot_count, tok_rows, 2).astype(jnp.float32), 2).astype(
        jnp.bfloat16
    )
    buffers = jnp.dot(dispatch_mat, normed, preferred_element_type=jnp.float32).astype(jnp.bfloat16)
    doubled = jnp.broadcast_to(
        buffers.reshape(experts, 1, capacity, model_width), (experts, 2, capacity, model_width)
    ).reshape(2 * experts, capacity, model_width)
    arrived = lax.all_to_all(doubled, "ep", split_axis=0, concat_axis=0, tiled=True)
    all_rows = lax.all_gather(arrived.reshape(-1, model_width), "pair", axis=0, tiled=True)
    gate_mat = w_gate[0]
    up_mat = w_up[0]
    down_mat = w_down[0]
    gated = jnp.dot(all_rows, gate_mat, preferred_element_type=jnp.float32)
    upward = jnp.dot(all_rows, up_mat, preferred_element_type=jnp.float32)
    active = (jax.nn.silu(gated) * upward).astype(jnp.bfloat16)
    halves = lax.psum_scatter(
        jnp.dot(active, down_mat, preferred_element_type=jnp.float32).astype(jnp.bfloat16),
        "pair",
        scatter_dimension=0,
        tiled=True,
    )
    returned = lax.all_to_all(
        halves.reshape(2 * experts, capacity, model_width),
        "ep",
        split_axis=0,
        concat_axis=0,
        tiled=True,
    )
    paired = returned.reshape(experts, 2, capacity, model_width)
    summed = (paired[:, 0].astype(jnp.float32) + paired[:, 1].astype(jnp.float32)).reshape(
        slot_count, model_width
    )
    combine_mat = jnp.sum(
        jnp.where(matches, gate_weights[0].reshape(-1)[None, :], 0.0).reshape(
            slot_count, tok_rows, 2
        ),
        2,
    )
    mixed_out = jnp.einsum("st,sd->td", combine_mat, summed, precision=lax.Precision.HIGHEST)
    resid = own_hidden + mixed_out
    velocity = jnp.dot(
        (rms_scale(resid) * final_gain).astype(jnp.bfloat16),
        w_out,
        preferred_element_type=jnp.float32,
    )
    own_latent = latent[0]
    outgoing = jnp.concatenate([velocity, own_latent], 1)
    incoming = from_partner(outgoing, "pair", 0)
    channels = velocity.shape[1]
    partner_vel = incoming[:, :channels]
    partner_latent = incoming[:, channels:]
    is_cond = lax.axis_index("pair") % 2 == 0
    cond_vel = jnp.where(is_cond, velocity, partner_vel)
    uncond_vel = jnp.where(is_cond, partner_vel, velocity)
    guided = uncond_vel + GUIDANCE * (cond_vel - uncond_vel)
    whole_latent = jnp.where(
        is_cond,
        jnp.concatenate([own_latent, partner_latent], 1),
        jnp.concatenate([partner_latent, own_latent], 1),
    )
    advanced = whole_latent + STEP_SIZE * guided
    half_width = own_latent.shape[1]
    own_next = jnp.where(is_cond, advanced[:, :half_width], advanced[:, half_width:])
    embedded = jnp.dot(advanced.astype(jnp.bfloat16), w_in, preferred_element_type=jnp.float32)
    modulated = (rms_scale(embedded) * modulation[0, 1] + modulation[0, 0]).astype(jnp.bfloat16)
    all_modulated = lax.all_gather(modulated, "pair", axis=0, tiled=True)
    local_cols = jnp.dot(all_modulated, w_qkv, preferred_element_type=jnp.float32).astype(
        jnp.bfloat16
    )
    projected = lax.all_to_all(local_cols, "pair", split_axis=0, concat_axis=1, tiled=True)
    head_width = projected.shape[1] // 3
    head_count = head_width // HDIM
    queries = projected[:, :head_width].reshape(tok_rows, head_count, HDIM)
    key_cols = projected[:, head_width : 2 * head_width]
    value_cols = projected[:, 2 * head_width :]
    score_scale = 1.0 / math.sqrt(HDIM)
    running_max = jnp.full((head_count, tok_rows), -1e30, jnp.float32)
    key_piece = lax.all_gather(key_cols, "ep", axis=0, tiled=True).reshape(-1, head_count, HDIM)
    value_piece = lax.all_gather(value_cols, "ep", axis=0, tiled=True).reshape(-1, head_count, HDIM)
    scores = (
        jnp.einsum("thd,nhd->htn", queries, key_piece, preferred_element_type=jnp.float32)
        * score_scale
    )
    new_max = jnp.maximum(running_max, jnp.max(scores, 2))
    weights = jnp.exp(scores - new_max[:, :, None])
    new_sum = jnp.sum(weights, 2)
    new_accum = jnp.einsum(
        "htn,nhd->htd", weights, value_piece.astype(jnp.float32), precision=lax.Precision.HIGHEST
    )
    attended = (
        (new_accum / new_sum[:, :, None])
        .transpose(1, 0, 2)
        .reshape(tok_rows, head_width)
        .astype(jnp.bfloat16)
    )
    return (own_next[None], attended[None])


Z_IN, X_IN, Y_IN, XY_IN, YX_IN, CORE_IN = 0, 1, 2, 3, 4, 5
CORE_OUT, XD_OUT, YD_OUT, X_OUT, Y_OUT, Z_OUT = 9, 10, 11, 12, 13, 14
KINDS = 15


def fused_kernel(
    hid_hbm,
    moe_gain_hbm,
    ids_hbm,
    gates_hbm,
    gate_hbm,
    up_hbm,
    down_hbm,
    final_gain_hbm,
    out_hbm,
    lat_hbm,
    in_hbm,
    mod_hbm,
    qkv_hbm,
    next_ref,
    att_ref,
    hid,
    moe_gain,
    ids,
    gates,
    final_gain,
    lat,
    rows,
    wg,
    wu,
    wd,
    wout,
    win,
    wqkv,
    act,
    sums,
    core_send,
    core_recv,
    diag_send,
    diag_recv,
    side_send,
    side_recv,
    z_send,
    z_recv,
    lats,
    mods,
    vels,
    cols,
    qkv,
    heads,
    whole,
    early_sem,
    load_sem,
    send_sem,
    recv_sem,
    small_send,
    small_recv,
    col_send,
    col_recv,
    head_send,
    head_recv,
):
    p, ep = lax.axis_index("pair"), lax.axis_index("ep")
    barrier = pltpu.get_barrier_semaphore()

    def greet(d, carry):
        other = lax.rem(p * 8 + ep + d, 32)
        pl.semaphore_signal(
            barrier,
            inc=1,
            device_id=(lax.div(other, 8), lax.rem(other, 8)),
            device_id_type=pl.DeviceIdType.MESH,
        )
        return carry

    early = [
        pltpu.make_async_copy(src, dst, early_sem.at[i])
        for i, (src, dst) in enumerate(
            (
                (hid_hbm, hid),
                (moe_gain_hbm, moe_gain),
                (ids_hbm, ids),
                (gates_hbm, gates),
                (final_gain_hbm, final_gain),
                (lat_hbm, lat),
                (mod_hbm.at[0], mods.at[0]),
            )
        )
    ]
    for load in early:
        load.start()
    lax.fori_loop(1, 32, greet, 0)
    x, y = lax.rem(p, 2), lax.div(p, 2)
    core, z = lax.rem(ep, 2), lax.div(ep, 2)
    px, py = y * 2 + (1 - x), (1 - y) * 2 + x
    pd = (1 - y) * 2 + (1 - x)
    pairs = (p, px, py, pd)
    core_ep = z * 2 + (1 - core)
    tok = hid.shape[1]
    half = tok // 2
    hidden_units = wg.shape[1]
    width = wd.shape[1]

    def place(k):
        low = lax.rem(lax.rem(z, 2) + lax.rem(k, 2), 2)
        high = lax.rem(lax.div(z, 2) + lax.div(k, 2), 2)
        return high * 2 + low

    def copy(src, dst, sent, received, device):
        return pltpu.make_async_remote_copy(
            src_ref=src,
            dst_ref=dst,
            send_sem=sent,
            recv_sem=received,
            device_id=device,
            device_id_type=pl.DeviceIdType.MESH,
        )

    top, low = pl.ds(0, half), pl.ds(half, half)

    def group(kind, k):
        if kind == Z_IN:
            src, dst, dev = rows.at[0, 0, 0], rows.at[k, 0, 0], (p, place(k) * 2 + core)
        elif kind == X_IN:
            src, dst, dev = rows.at[k, 0, 0], rows.at[k, 0, 1], (px, ep)
        elif kind == Y_IN:
            src, dst, dev = rows.at[k, 0, 0], rows.at[k, 0, 2], (py, ep)
        elif kind == XY_IN:
            src, dst, dev = rows.at[k, 0, 1, top], rows.at[k, 0, 3, top], (py, ep)
        elif kind == YX_IN:
            src, dst, dev = rows.at[k, 0, 2, low], rows.at[k, 0, 3, low], (px, ep)
        elif kind < CORE_OUT:
            r = kind - CORE_IN
            src, dst, dev = rows.at[k, 0, r], rows.at[k, 1, r], (p, core_ep)
        elif kind == CORE_OUT:
            src, dst, dev = core_send.at[k], core_recv.at[k], (p, core_ep)
        elif kind == XD_OUT:
            src, dst, dev = diag_send.at[k, 0], diag_recv.at[k, 0], (px, ep)
        elif kind == YD_OUT:
            src, dst, dev = diag_send.at[k, 1], diag_recv.at[k, 1], (py, ep)
        elif kind == X_OUT:
            src, dst, dev = side_send.at[k, 0], side_recv.at[k, 0], (px, ep)
        elif kind == Y_OUT:
            src, dst, dev = side_send.at[k, 1], side_recv.at[k, 1], (py, ep)
        else:
            src, dst, dev = z_send.at[k], z_recv.at[k], (p, place(k) * 2 + core)
        return copy(src, dst, send_sem.at[kind, k], recv_sem.at[kind, k], dev)

    loads = [
        pltpu.make_async_copy(src, dst, load_sem.at[i])
        for i, (src, dst) in enumerate(
            (
                (gate_hbm.at[0], wg),
                (up_hbm.at[0], wu),
                (down_hbm.at[0], wd),
                (out_hbm, wout),
                (in_hbm, win),
                (qkv_hbm, wqkv),
            )
        )
    ]

    for load in loads:
        load.start()
    for load in early:
        load.wait()
    rows[0, 0, 0] = (rms_scale(hid[0]) * moe_gain[...]).astype(jnp.bfloat16)
    lats[0] = jnp.zeros_like(lats[0])
    lats[0, :, : lat.shape[2]] = lat[0]
    pl.semaphore_wait(barrier, 31)

    def small(kind, r):
        buffer = (lats, mods, vels)[kind]
        return copy(
            buffer.at[0],
            buffer.at[r],
            small_send.at[kind, r],
            small_recv.at[kind, r],
            (pairs[r], ep),
        )

    def spread(k):
        @pl.when(k > 0)
        def _():
            group(Z_IN, k).wait_recv()

        group(X_IN, k).start()
        group(Y_IN, k).start()

        @pl.when(k == 0)
        def _():
            group(Z_IN, 1).start()
            group(Z_IN, 2).start()

        group(CORE_IN, k).start()

    def forward(k):
        group(X_IN, k).wait_recv()
        group(XY_IN, k).start()
        group(CORE_IN + 1, k).start()
        group(Y_IN, k).wait_recv()
        group(YX_IN, k).start()
        group(CORE_IN + 2, k).start()

    def experts(k):
        group(XY_IN, k).wait_recv()
        group(YX_IN, k).wait_recv()
        group(CORE_IN + 3, k).start()
        for r in range(4):
            group(CORE_IN + r, k).wait_recv()

        @pl.when(k == 1)
        def _():
            for load in loads[:3]:
                load.wait()

        own = rows[k].reshape(8 * tok, width)
        step = min(256, hidden_units)
        for at in range(0, hidden_units, step):
            gated = jnp.dot(own, wg[:, at : at + step], preferred_element_type=jnp.float32)
            upward = jnp.dot(own, wu[:, at : at + step], preferred_element_type=jnp.float32)
            act[:, at : at + step] = (jax.nn.silu(gated) * upward).astype(jnp.bfloat16)
        step = min(512, width)
        for at in range(0, width, step):
            part = jnp.dot(act[...], wd[:, at : at + step], preferred_element_type=jnp.float32)
            part = part.reshape(2, 4, tok, step)
            sums[k, :, :, at : at + step] = part[0]
            core_send[k, :, :, at : at + step] = part[1].astype(jnp.bfloat16)
        group(CORE_OUT, k).start()

    def join_cores(k):
        group(CORE_OUT, k).wait_recv()
        diag = sums[k, 3] + core_recv[k, 3].astype(jnp.float32)
        diag_send[k] = diag.astype(jnp.bfloat16).reshape(2, half, width)
        group(XD_OUT, k).start()
        group(YD_OUT, k).start()
        for r in range(3):
            sums[k, r] = sums[k, r] + core_recv[k, r].astype(jnp.float32)

    def join_diagonal(k):
        group(XD_OUT, k).wait_recv()
        group(YD_OUT, k).wait_recv()
        side_send[k, 0, :half] = sums[k, 1, :half].astype(jnp.bfloat16)
        side_send[k, 0, half:] = (
            sums[k, 1, half:] + diag_recv[k, 1].astype(jnp.float32)
        ).astype(jnp.bfloat16)
        group(X_OUT, k).start()
        side_send[k, 1, :half] = (
            sums[k, 2, :half] + diag_recv[k, 0].astype(jnp.float32)
        ).astype(jnp.bfloat16)
        side_send[k, 1, half:] = sums[k, 2, half:].astype(jnp.bfloat16)
        group(Y_OUT, k).start()

    def join_sides(k):
        group(X_OUT, k).wait_recv()
        group(Y_OUT, k).wait_recv()
        total = (
            sums[k, 0]
            + side_recv[k, 0].astype(jnp.float32)
            + side_recv[k, 1].astype(jnp.float32)
        ).astype(jnp.bfloat16)

        @pl.when(k == 0)
        def _():
            z_recv[0] = total

        @pl.when(k > 0)
        def _():
            z_send[k] = total
            group(Z_OUT, k).start()

    spread(0)
    for r in range(1, 4):
        small(0, r).start()
        small(1, r).start()
    forward(0)
    group(Z_IN, 3).start()
    spread(1)
    spread(2)

    forward(1)

    def turn(i, carry):
        @pl.when(i == 1)
        def _():
            spread(3)
            forward(2)

        @pl.when(i == 2)
        def _():
            forward(3)

        @pl.when(i >= 1)
        def _():
            join_cores(i)

        experts(lax.rem(i + 1, 4))

        @pl.when(i >= 2)
        def _():
            join_sides(i - 1)

        @pl.when(i >= 1)
        def _():
            join_diagonal(i)

        return carry

    lax.fori_loop(0, 4, turn, 0)
    join_cores(0)
    join_sides(3)
    join_diagonal(0)
    join_sides(0)

    mixed = jnp.zeros((tok, width), jnp.float32)
    eye = lax.broadcasted_iota(jnp.int32, (tok, tok), 0) == lax.broadcasted_iota(
        jnp.int32, (tok, tok), 1
    )
    for k in range(4):
        if k > 0:
            group(Z_OUT, k).wait_recv()
        weight = jnp.sum(jnp.where(ids[0] == place(k), gates[0], 0.0), 0, keepdims=True)
        weight = jnp.sum(jnp.where(eye, weight, 0.0), 1, keepdims=True)
        mixed = mixed + weight * z_recv[k].astype(jnp.float32)
    resid = hid[0] + mixed
    loads[3].wait()
    vels[0] = jnp.dot(
        (rms_scale(resid) * final_gain[...]).astype(jnp.bfloat16),
        wout[...],
        preferred_element_type=jnp.float32,
    )
    for r in range(1, 4):
        small(2, r).start()
    for kind in range(3):
        for r in range(1, 4):
            small(kind, r).wait_recv()

    is_cond = x == 0
    half_channels = lat.shape[2]

    def advance(first, second):
        cond_vel = jnp.where(is_cond, vels[first], vels[second])
        uncond_vel = jnp.where(is_cond, vels[second], vels[first])
        cond_lat = jnp.where(is_cond, lats[first], lats[second])[:, :half_channels]
        uncond_lat = jnp.where(is_cond, lats[second], lats[first])[:, :half_channels]
        guided = uncond_vel + GUIDANCE * (cond_vel - uncond_vel)
        return jnp.concatenate([cond_lat, uncond_lat], 1) + STEP_SIZE * guided

    advanced = advance(0, 1)
    next_ref[0] = jnp.where(is_cond, advanced[:, :half_channels], advanced[:, half_channels:])
    both = jnp.concatenate([advanced, advance(2, 3)], 0).astype(jnp.bfloat16)
    loads[4].wait()
    scaled = rms_scale(jnp.dot(both, win[...], preferred_element_type=jnp.float32))
    modulated = jnp.concatenate(
        [
            (scaled[(r // 2) * tok : (r // 2 + 1) * tok] * mods[r, 1:2] + mods[r, 0:1]).astype(
                jnp.bfloat16
            )
            for r in range(4)
        ],
        0,
    )
    loads[5].wait()
    local = jnp.dot(modulated, wqkv[...], preferred_element_type=jnp.float32).astype(jnp.bfloat16)
    blocks = local.shape[1] // HDIM
    for r in range(4):
        for b in range(blocks):
            cols[r, b] = local[r * tok : (r + 1) * tok, b * HDIM : (b + 1) * HDIM]

    def column(r, b):
        number = p * blocks + b
        sort, head = lax.div(number, 8), lax.rem(number, 8)
        return head, sort, copy(
            cols.at[r, b],
            qkv.at[sort, ep],
            col_send.at[r, b],
            col_recv.at[sort, ep],
            (pairs[r], head),
        )

    def each_column(act_on, keep):
        for r in (3, 1, 2, 0):
            for b in range(blocks):
                head, sort, moved = column(r, b)
                if r > 0:
                    act_on(moved)
                    continue

                @pl.when(head != ep)
                def _(moved=moved):
                    act_on(moved)

                if keep:

                    @pl.when(head == ep)
                    def _(sort=sort, b=b):
                        qkv[sort, ep] = cols[0, b]

    each_column(lambda moved: moved.start(), True)
    for sort in range(3):
        for j in range(8):

            @pl.when((lax.div(sort * 8 + ep, blocks) != p) | (ep != j))
            def _(sort=sort, j=j):
                copy(
                    qkv.at[sort, j],
                    qkv.at[sort, j],
                    col_send.at[0, 0],
                    col_recv.at[sort, j],
                    (px, ep),
                ).wait_recv()

    query, key, value = (qkv[sort].reshape(8 * tok, HDIM) for sort in range(3))
    scores = lax.dot_general(
        query, key, (((1,), (1,)), ((), ())), preferred_element_type=jnp.float32
    ) * (1.0 / math.sqrt(HDIM))
    weights = jnp.exp(scores - jnp.max(scores, 1, keepdims=True))
    total = jnp.sum(weights, 1, keepdims=True)
    mixed_values = jnp.dot(
        weights.astype(jnp.bfloat16), value, preferred_element_type=jnp.float32
    )
    heads[...] = (mixed_values / total).astype(jnp.bfloat16).reshape(8, tok, HDIM)

    def result(d):
        j = lax.rem(ep + d, 8)
        return copy(heads.at[j], whole.at[ep], head_send.at[d], head_recv.at[d], (p, j))

    for d in range(1, 8):
        result(d).start()
    whole[ep] = heads[ep]
    for d in range(1, 8):
        j = lax.rem(ep + 8 - d, 8)
        copy(whole.at[j], whole.at[j], head_send.at[d], head_recv.at[d], (px, ep)).wait_recv()
    for h in range(8):
        att_ref[0, :, h * HDIM : (h + 1) * HDIM] = whole[h]

    def settle(k, carry):
        for kind in range(KINDS):
            if kind in (Z_IN, Z_OUT):

                @pl.when(k > 0)
                def _(kind=kind):
                    group(kind, k).wait_send()

            else:
                group(kind, k).wait_send()
        return carry

    lax.fori_loop(0, 4, settle, 0)
    for kind in range(3):
        for r in range(1, 4):
            small(kind, r).wait_send()
    each_column(lambda moved: moved.wait_send(), False)
    for d in range(1, 8):
        result(d).wait_send()


def fused(
    hidden,
    moe_gain,
    expert_ids,
    gate_weights,
    w_gate,
    w_up,
    w_down,
    final_gain,
    w_out,
    latent,
    w_in,
    modulation,
    w_qkv,
):
    tok, width = hidden.shape[1:]
    units = w_gate.shape[2]
    channels = w_out.shape[1]
    columns = w_qkv.shape[1]
    blocks = columns // HDIM
    b16, f32 = jnp.bfloat16, jnp.float32
    vmem, hbm = pl.BlockSpec(memory_space=pltpu.VMEM), pl.BlockSpec(memory_space=pl.ANY)
    dma = pltpu.SemaphoreType.DMA
    half = tok // 2
    return pl.pallas_call(
        fused_kernel,
        out_shape=(
            jax.ShapeDtypeStruct(latent.shape, f32),
            jax.ShapeDtypeStruct((1, tok, 8 * HDIM), b16),
        ),
        in_specs=[hbm] * 13,
        out_specs=(vmem, vmem),
        scratch_shapes=[
            pltpu.VMEM(hidden.shape, f32),
            pltpu.VMEM((1, width), f32),
            pltpu.VMEM((1, 2, tok), jnp.int32),
            pltpu.VMEM((1, 2, tok), f32),
            pltpu.VMEM((1, width), f32),
            pltpu.VMEM(latent.shape, f32),
            pltpu.VMEM((4, 2, 4, tok, width), b16),
            pltpu.VMEM((width, units), b16),
            pltpu.VMEM((width, units), b16),
            pltpu.VMEM((units, width), b16),
            pltpu.VMEM(w_out.shape, b16),
            pltpu.VMEM(w_in.shape, b16),
            pltpu.VMEM(w_qkv.shape, b16),
            pltpu.VMEM((8 * tok, units), b16),
            pltpu.VMEM((4, 4, tok, width), f32),
            pltpu.VMEM((4, 4, tok, width), b16),
            pltpu.VMEM((4, 4, tok, width), b16),
            pltpu.VMEM((4, 2, half, width), b16),
            pltpu.VMEM((4, 2, half, width), b16),
            pltpu.VMEM((4, 2, tok, width), b16),
            pltpu.VMEM((4, 2, tok, width), b16),
            pltpu.VMEM((4, tok, width), b16),
            pltpu.VMEM((4, tok, width), b16),
            pltpu.VMEM((4, tok, channels), f32),
            pltpu.VMEM((4, 2, width), f32),
            pltpu.VMEM((4, tok, channels), f32),
            pltpu.VMEM((4, blocks, tok, HDIM), b16),
            pltpu.VMEM((3, 8, tok, HDIM), b16),
            pltpu.VMEM((8, tok, HDIM), b16),
            pltpu.VMEM((8, tok, HDIM), b16),
            dma((7,)),
            dma((6,)),
            dma((KINDS, 4)),
            dma((KINDS, 4)),
            dma((3, 4)),
            dma((3, 4)),
            dma((4, blocks)),
            dma((3, 8)),
            dma((8,)),
            dma((8,)),
        ],
        compiler_params=pltpu.CompilerParams(
            collective_id=0, has_side_effects=True, vmem_limit_bytes=60 * 2**20
        ),
        name="guided_step",
    )(
        hidden,
        moe_gain[None],
        expert_ids.transpose(0, 2, 1),
        gate_weights.transpose(0, 2, 1),
        w_gate,
        w_up,
        w_down,
        final_gain[None],
        w_out,
        latent,
        w_in,
        modulation,
        w_qkv,
    )


def choose(mesh):
    if mesh.shape["pair"] == 4 and mesh.shape["ep"] == 8:
        return fused
    return per_device


def solution(mesh):
    return jax.shard_map(
        choose(mesh),
        mesh=mesh,
        in_specs=(
            P("pair", "ep", None),
            P(),
            P("pair", "ep", None),
            P("pair", "ep", None),
            P("ep", None, "pair"),
            P("ep", None, "pair"),
            P("ep", "pair", None),
            P(),
            P(),
            P("pair", "ep", None),
            P(),
            P("pair", None, None),
            P(None, "pair"),
        ),
        out_specs=(P("pair", "ep", None), P("pair", "ep", None)),
        check_vma=False,
    )
```
